128 devices in a mesh: pair: 4 (over z), node: 32 (over x, y, core).
Axes of the slice: x: 4, y: 4, z: 4, core: 2. Of those that a mesh axis runs over, the one named last changes fastest.
Arguments:
- node_feats: bfloat16 [4096, 1024], P('node'), may hold values from -6 to 6
- msg_weight: bfloat16 [1024, 1024], replicated, may hold values from -0.1875 to 0.1875
- msg_bias: float32 [1024], replicated, may hold values from -3 to 3
- edge_source: int32 [8192], P('node'), may hold values from 0 to 127
- edge_slot: int32 [8192], P('node'), may hold values from 0 to 511, as said below
- edge_target: int32 [8192], P('node'), may hold values from 0 to 127
- edge_weight: bfloat16 [8192], P('node'), may hold values from 0.25 to 4
- update_weight: bfloat16 [2048, 1024], replicated, may hold values from -0.125 to 0.125
- update_bias: float32 [1024], replicated, may hold values from -3 to 3
- pair_ids: int32 [8192, 2], P(('pair', 'node')), may hold values from 0 to 4095, as said below
- neg_ids: int32 [8192, 15], P(('pair', 'node')), may hold values from 0 to 4095, as said below
- hidden_weight: bfloat16 [3072, 1024], replicated, may hold values from -0.109375 to 0.109375
- hidden_bias: float32 [1024], replicated, may hold values from -3 to 3
- score_weight: bfloat16 [1024], replicated, may hold values from -0.1875 to 0.1875
- score_grad: float32 [8192, 16], P(('pair', 'node')), may hold values from -0.625 to 0.625
Outputs:
- embedding: bfloat16 [4096, 1024], P('node')
- scores: float32 [8192, 16], P(('pair', 'node'))
- grad_hidden_weight: float32 [3072, 1024], P(('pair', 'node'))
- grad_hidden_bias: float32 [1024], P(('pair', 'node'))
- grad_score_weight: float32 [1024], P(('pair', 'node'))
The draws below stay inside these ranges and needn't reach their ends.
Inputs may be any that keep to these rules, and one draw needn't show every extreme that they name: `edge_slot`: the 256 edges of one index of node (aligned blocks) take distinct slots; slot // 16 names the owner of the edge's destination, so one device sends at most 16 edges to one owner, and some owner receives exactly 16 from every device. Global node ids. Among the ids of pair_ids and neg_ids of one device's 64 pairs (aligned blocks) at most 68 fall in one owner's range of 128 ids (id // 128), and exactly 68 for some owner on every device. `neg_ids`: global node ids, with the bound stated for pair_ids on the same pairs.
All inputs are finite; a program needn't handle non-finite values.
Results may differ from the reference program's by a relative error of at most 0.025.
Values may be sent and summed in bfloat16 or wider, within the bound.
A program may use at most 128 MiB of HBM per device.

```python
import math
import jax
import jax.numpy as jnp
from jax import lax

D = 1024
H = 1024
NODE_DEV = 128
EDGES_DEV = 256
PAIRS_DEV = 64
NEG = 15
NODES = 4096
EDGES = 8192
CAP = 16
PAIRS = 8192
RCAP = 68
N_NODE = 32
DEVICES = 128


def pick_slots(key, owners, per_owner, taken_count, hot_owner, owner_bias):
    key_perm, key_extra, key_order = jax.random.split(key, 3)
    slot_total = owners * per_owner
    shuffled = jax.random.permutation(key_perm, slot_total)
    owner_ids = jnp.arange(slot_total) // per_owner
    own_extra = jax.random.randint(key_extra, (), 0, owners)
    forced = (owner_ids == hot_owner) | (owner_ids == own_extra)
    ranking = jnp.where(forced, shuffled - slot_total, owner_bias[owner_ids] * slot_total + shuffled)
    ordered = jnp.argsort(ranking, stable=True)[:taken_count]
    return jax.random.permutation(key_order, ordered).astype(jnp.int32)


def request_ids(key):
    key_hot, key_bias, key_rows, key_local = jax.random.split(key, 4)
    taken_count = PAIRS_DEV * (2 + NEG)
    hot_owner = jax.random.randint(key_hot, (), 0, N_NODE)
    owner_bias = jax.random.randint(key_bias, (N_NODE,), 0, 4)
    block_keys = jax.random.split(key_rows, DEVICES)
    chosen = jax.vmap(lambda k: pick_slots(k, N_NODE, RCAP, taken_count, hot_owner, owner_bias))(block_keys)
    local_ids = jax.random.randint(key_local, (DEVICES, taken_count), 0, NODE_DEV)
    return (chosen // RCAP * NODE_DEV + local_ids).astype(jnp.int32)


def draw_edge_slot(key, part):
    key = jax.random.fold_in(key, 11)
    key_hot, key_bias, key_rows = jax.random.split(key, 3)
    hot_owner = jax.random.randint(key_hot, (), 0, N_NODE)
    owner_bias = jax.random.randint(key_bias, (N_NODE,), 0, 4)
    block_keys = jax.random.split(key_rows, N_NODE)
    blocks = jax.vmap(lambda k: pick_slots(k, N_NODE, CAP, EDGES_DEV, hot_owner, owner_bias))(block_keys)
    return blocks.reshape(EDGES)


def draw_pair_ids(key, part):
    every_id = request_ids(key)
    return every_id[:, :2 * PAIRS_DEV].reshape(DEVICES * PAIRS_DEV, 2)


def draw_neg_ids(key, part):
    every_id = request_ids(key)
    return every_id[:, 2 * PAIRS_DEV:].reshape(DEVICES * PAIRS_DEV, NEG)


def place_ends(values, key, least, largest):
    longest = values.shape.index(max(values.shape))
    spots = []
    for shift in (0, 1):
        where = [jax.random.randint(jax.random.fold_in(key, axis), (), 0, length) for axis, length in enumerate(values.shape)]
        where[longest] = (where[longest] + shift) % values.shape[longest]
        spots.append(tuple(where))
    return values.at[spots[0]].set(least).at[spots[1]].set(largest)


def block_scale(key, extent, cuts, smallest, top_value):
    level, own = 1.0, jax.random.fold_in(key, 6)
    for dim, shards_of in cuts:
        heights = jnp.exp(jax.random.uniform(jax.random.fold_in(own, dim), (shards_of,), jnp.float32, smallest / len(cuts), top_value / len(cuts)))
        level = level * jnp.repeat(heights, extent[dim] // shards_of).reshape([-1 if axis == dim else 1 for axis in range(len(extent))])
    return level


def gaussian(rng, dims, deviation, reach, shards=(), kind=jnp.bfloat16):
    array = jax.random.normal(rng, dims, jnp.float32) * deviation
    if len(shards) > 0:
        array = block_scale(rng, dims, shards, -0.22, 0.18) * array
    return jnp.clip(array, min=-reach, max=reach).astype(kind)


def setup_inputs(seed: int = 0) -> dict:
    streams_of = jax.random.split(jax.random.key(seed), 16)
    node_feats = gaussian(streams_of[0], (NODES, D), 1.0, 6.0, ((0, 32),))
    msg_weight = gaussian(streams_of[1], (D, D), D ** -0.5, 0.1875)
    msg_bias = gaussian(streams_of[2], (D,), 0.5, 3.0, (), jnp.float32)
    edge_source = place_ends(jax.random.randint(streams_of[3], (EDGES,), 0, NODE_DEV), jax.random.fold_in(streams_of[3], 1), 0, NODE_DEV - 1).astype(jnp.int32)
    edge_slot = draw_edge_slot(jax.random.fold_in(streams_of[15], 71), 0)
    edge_target = place_ends(jax.random.randint(streams_of[5], (EDGES,), 0, NODE_DEV), jax.random.fold_in(streams_of[5], 1), 0, NODE_DEV - 1).astype(jnp.int32)
    edge_weight = jnp.clip(jnp.exp(math.log(4.0) - 2.7725887 * jax.random.uniform(streams_of[6], (EDGES,), jnp.float32) ** block_scale(streams_of[6], (EDGES,), ((0, 32),), -0.2, 0.2)), 0.25, 4.0).astype(jnp.bfloat16)
    update_weight = gaussian(streams_of[7], (2 * D, D), (2 * D) ** -0.5, 0.125)
    update_bias = gaussian(streams_of[8], (D,), 0.5, 3.0, (), jnp.float32)
    pair_ids = draw_pair_ids(jax.random.fold_in(streams_of[15], 71), 0)
    neg_ids = draw_neg_ids(jax.random.fold_in(streams_of[15], 71), 0)
    hidden_weight = gaussian(streams_of[11], (3 * D, H), (3 * D) ** -0.5, 0.109375)
    hidden_bias = gaussian(streams_of[12], (H,), 0.5, 3.0, (), jnp.float32)
    score_weight = gaussian(streams_of[13], (H,), H ** -0.5, 0.1875)
    score_grad = gaussian(streams_of[14], (PAIRS, 1 + NEG), (16.0 / (PAIRS * (1 + NEG)) ** 0.5), 0.625, ((0, 128),), jnp.float32)
    return {"node_feats": node_feats, "msg_weight": msg_weight, "msg_bias": msg_bias, "edge_source": edge_source, "edge_slot": edge_slot, "edge_target": edge_target, "edge_weight": edge_weight, "update_weight": update_weight, "update_bias": update_bias, "pair_ids": pair_ids, "neg_ids": neg_ids, "hidden_weight": hidden_weight, "hidden_bias": hidden_bias, "score_weight": score_weight, "score_grad": score_grad}


def pair_block(embedding, pair_rows, neg_rows, hidden_weight, hidden_bias, score_weight, score_cot):
    query_rows = embedding[pair_rows[:, 0]]
    positive = embedding[pair_rows[:, 1]]
    negatives = embedding[neg_rows]
    cand_rows = jnp.concatenate([positive[:, None, :], negatives], axis=1)
    query_full = jnp.broadcast_to(query_rows[:, None, :], cand_rows.shape)
    product = (query_full.astype(jnp.float32) * cand_rows.astype(jnp.float32)).astype(jnp.bfloat16)
    inputs = jnp.concatenate([query_full, cand_rows, product], axis=-1).reshape(-1, 3 * query_rows.shape[1])
    pre_act = jnp.dot(inputs, hidden_weight, preferred_element_type=jnp.float32) + hidden_bias
    sigmoid_pre = jax.nn.sigmoid(pre_act)
    hidden = (pre_act * sigmoid_pre).astype(jnp.bfloat16)
    scores = jnp.dot(hidden, score_weight, preferred_element_type=jnp.float32)
    cot_flat = score_cot.reshape(-1)
    grad_score = lax.optimization_barrier(jnp.sum(cot_flat[:, None] * hidden.astype(jnp.float32), axis=0))
    hidden_grad = cot_flat[:, None] * score_weight.astype(jnp.float32)[None, :]
    pre_grad = (hidden_grad * sigmoid_pre * (1.0 + pre_act * (1.0 - sigmoid_pre))).astype(jnp.bfloat16)
    grad_bias = lax.optimization_barrier(jnp.sum(pre_grad.astype(jnp.float32), axis=0))
    grad_weight = lax.dot_general(inputs, pre_grad, (((0,), (0,)), ((), ())), preferred_element_type=jnp.float32)
    return (scores.reshape(pair_rows.shape[0], -1), grad_weight, grad_bias, grad_score)

def reference(node_feats, msg_weight, msg_bias, edge_source, edge_slot, edge_target, edge_weight, update_weight, update_bias, pair_ids, neg_ids, hidden_weight, hidden_bias, score_weight, score_grad):
    project = jax.nn.relu(jnp.dot(node_feats, msg_weight, preferred_element_type=jnp.float32) + msg_bias)
    device = (jnp.arange(EDGES, dtype=jnp.int32) // EDGES_DEV).astype(jnp.int32)
    source = (device * NODE_DEV + edge_source).astype(jnp.int32)
    target = (edge_slot // CAP * NODE_DEV + edge_target).astype(jnp.int32)
    weight_f = edge_weight.astype(jnp.float32)
    message = (weight_f[:, None] * project[source]).astype(jnp.bfloat16)
    sums = jax.ops.segment_sum(message.astype(jnp.float32), target, NODES)
    totals = jax.ops.segment_sum(weight_f, target, NODES)
    average = (sums / jnp.maximum(totals, 1.0)[:, None]).astype(jnp.bfloat16)
    joined = jnp.concatenate([node_feats, average], axis=1)
    rectified = jax.nn.relu(jnp.dot(joined, update_weight, preferred_element_type=jnp.float32) + update_bias)
    embedding = (rectified * lax.rsqrt(lax.optimization_barrier(jnp.mean(rectified * rectified, axis=-1, keepdims=True)) + 1e-06)).astype(jnp.bfloat16)
    pair_blocks = pair_ids.reshape(DEVICES, PAIRS_DEV, 2)
    neg_blocks = neg_ids.reshape(DEVICES, PAIRS_DEV, NEG)
    cot_blocks = score_grad.reshape(DEVICES, PAIRS_DEV, 1 + NEG)

    def block_step(running, blocks):
        block_scores, grad_weight, grad_bias, grad_score = pair_block(embedding, blocks[0], blocks[1], hidden_weight, hidden_bias, score_weight, blocks[2])
        return ((running[0] + grad_weight, running[1] + grad_bias, running[2] + grad_score), block_scores)
    start = (jnp.zeros((3 * D, H), jnp.float32), jnp.zeros((H,), jnp.float32), jnp.zeros((H,), jnp.float32))
    grads, all_scores = lax.scan(block_step, start, (pair_blocks, neg_blocks, cot_blocks))
    scores = all_scores.reshape(PAIRS, 1 + NEG)
    return (embedding, scores, grads[0], grads[1], grads[2])
```

```python
import functools
import jax
import jax.numpy as jnp
from jax import lax
from jax.experimental import pallas as pl
from jax.experimental.pallas import tpu as pltpu
from jax.sharding import PartitionSpec as P

MESH = pl.DeviceIdType.MESH
F32 = jnp.float32
BF16 = jnp.bfloat16
ORDERS = (("z", "x", "y"), ("x", "y", "z"), ("y", "z", "x"))


def place():
    node = lax.axis_index("node")
    return {
        "z": lax.axis_index("pair"),
        "x": node // 8,
        "y": (node // 2) % 4,
        "c": node % 2,
    }


def device(at, **other):
    pos = dict(at, **other)
    return (pos["z"], pos["x"] * 8 + pos["y"] * 2 + pos["c"])


def ring(at, axis, step):
    return device(at, **{axis: (at[axis] + step) % 4})


def part(ref, third, **sel):
    full = pl.ds(0, 4)
    return ref.at[sel.get("z", full), sel.get("x", full), sel.get("y", full), third]


def spot(n):
    chip = n // 3
    return (chip // 16, (chip // 4) % 4, chip % 4, n % 3)


class Links:
    def __init__(self, send_sem, recv_sem):
        self.send_sem, self.recv_sem, self.count, self.copies = send_sem, recv_sem, 0, []

    def start(self, src, dst, to):
        copy = pltpu.make_async_remote_copy(
            src_ref=src,
            dst_ref=dst,
            send_sem=self.send_sem.at[self.count],
            recv_sem=self.recv_sem.at[self.count],
            device_id=to,
            device_id_type=MESH,
        )
        copy.start()
        self.count += 1
        self.copies.append(copy)
        return copy

    def drop(self, done):
        self.copies = [copy for copy in self.copies if copy is not done]

    def drain(self):
        for copy in self.copies:
            copy.wait_send()


def meet(partners):
    barrier = pltpu.get_barrier_semaphore()
    for to in partners:
        pl.semaphore_signal(barrier, inc=1, device_id=to, device_id_type=MESH)
    pl.semaphore_wait(barrier, len(partners))


def add_into(dst, *srcs):
    total = dst[...].astype(F32)
    for src in srcs:
        total = total + src[...].astype(F32)
    dst[...] = total.astype(dst.dtype)


def score_kernel(
    q_ref, cand_ref, hw_ref, hb_ref, sw_ref, sg_ref,
    scores_ref, gw_ref, aux_out_ref,
    q2, gq2, prod, grad, query_act, acc_bias, acc_score,
    own, give, take,
    opp1, near1, opp2, near2, last3, final, final_in,
    aux, aux_core, aux_in,
    core_send, core_recv, send_sem, recv_sem,
):
    at = place()
    core = at["c"]
    partners = [device(at, c=1 - core)]
    for axis in ("x", "y", "z"):
        for step in (1, 2, 3):
            partners.append(ring(at, axis, step))
    meet(partners)
    sibling = partners[0]
    links = Links(send_sem, recv_sem)

    query = q_ref[...]
    q2[pl.ds(0, 64)] = query
    q2[pl.ds(64, 64)] = query
    query_act[...] = jnp.dot(query, hw_ref[pl.ds(0, 1024)], preferred_element_type=F32) + hb_ref[...]
    acc_bias[...] = jnp.zeros_like(acc_bias)
    acc_score[...] = jnp.zeros_like(acc_score)
    scores_ref[...] = jnp.zeros_like(scores_ref)

    def forward(i, query_grad):
        rows = pl.ds(pl.multiple_of(i * 256, 256), 256)
        cand = cand_ref[rows]
        query = q_ref[...]
        product = (cand.astype(F32).reshape(4, 64, 1024) * query.astype(F32)[None]).astype(BF16).reshape(256, 1024)
        prod[rows] = product
        act = jnp.dot(cand, hw_ref[pl.ds(1024, 1024)], preferred_element_type=F32)
        act = act + jnp.dot(product, hw_ref[pl.ds(2048, 1024)], preferred_element_type=F32)
        sw = sw_ref[...].astype(F32)
        sg = sg_ref[...]
        lane = lax.broadcasted_iota(jnp.int32, (64, 16), 1)
        score = scores_ref[...]
        bias_sum = acc_bias[...]
        score_sum = acc_score[...]
        for k in range(4):
            mine = lane == i * 4 + k
            x = act[k * 64 : (k + 1) * 64] + query_act[...]
            s = 0.5 * jnp.tanh(0.5 * x) + 0.5
            hidden = (x * s).astype(BF16).astype(F32)
            score = score + jnp.where(mine, jnp.sum(hidden * sw, axis=1, keepdims=True), 0.0)
            cot = jnp.sum(jnp.where(mine, sg, 0.0), axis=1, keepdims=True)
            score_sum = score_sum + jnp.sum((cot * hidden).reshape(8, 8, 1024), axis=0)
            pre_grad = (cot * sw * s * (1.0 + x * (1.0 - s))).astype(BF16)
            grad[pl.ds(pl.multiple_of(i * 256 + k * 64, 64), 64)] = pre_grad
            pre_grad = pre_grad.astype(F32)
            bias_sum = bias_sum + jnp.sum(pre_grad.reshape(8, 8, 1024), axis=0)
            query_grad = query_grad + pre_grad
        scores_ref[...] = score
        acc_bias[...] = bias_sum
        acc_score[...] = score_sum
        return query_grad

    query_grad = lax.fori_loop(0, 4, forward, jnp.zeros((64, 1024), F32))
    high = query_grad.astype(BF16)
    gq2[pl.ds(0, 64)] = high
    gq2[pl.ds(64, 64)] = (query_grad - high.astype(F32)).astype(BF16)
    aux[pl.ds(0, 1)] = jnp.sum(acc_bias[...], axis=0, keepdims=True)
    aux[pl.ds(1, 1)] = jnp.sum(acc_score[...], axis=0, keepdims=True)
    aux_core_copy = links.start(aux, aux_core, sibling)

    def core_copy(j):
        blocks = pl.ds(j * 16, 16)
        return pltpu.make_async_remote_copy(
            src_ref=give.at[blocks],
            dst_ref=take.at[blocks],
            send_sem=core_send.at[j],
            recv_sem=core_recv.at[j],
            device_id=sibling,
            device_id_type=MESH,
        )

    my_cols = pl.ds(pl.multiple_of(core * 512, 512), 512)
    other_cols = pl.ds(pl.multiple_of((1 - core) * 512, 512), 512)
    contract = (((0,), (0,)), ((), ()))

    def chunk(j, x_ref, g_ref, k):
        x = x_ref[:, pl.ds(pl.multiple_of(k * 256, 256), 256)]
        other = lax.dot_general(x, g_ref[:, other_cols], contract, preferred_element_type=F32)
        give[pl.ds(j * 16, 16)] = other.astype(BF16).reshape(16, 16, 512)
        core_copy(j).start()
        mine = lax.dot_general(x, g_ref[:, my_cols], contract, preferred_element_type=F32)
        mine = mine.astype(BF16)
        for b in range(16):
            own[spot(j * 16 + b)] = mine[b * 16 : (b + 1) * 16]

    def land(j):
        core_copy(j).wait_recv()
        for b in range(16):
            n = j * 16 + b
            own[spot(n)] = (own[spot(n)].astype(F32) + take[n].astype(F32)).astype(BF16)

    def weight_c(k, carry):
        chunk(k + 4, cand_ref, grad, k)
        return carry

    def weight_p(k, carry):
        chunk(k + 8, prod, grad, k)
        land(k + 4)
        return carry

    def weight_q(k, carry):
        chunk(k, q2, gq2, k)
        land(k + 8)
        return carry

    def weight_last(k, carry):
        land(k)
        return carry

    lax.fori_loop(0, 4, weight_c, 0)
    lax.fori_loop(0, 4, weight_p, 0)
    lax.fori_loop(0, 4, weight_q, 0)
    aux_core_copy.wait()
    links.drop(aux_core_copy)
    add_into(aux, aux_core)
    lax.fori_loop(0, 4, weight_last, 0)

    low, high_half = pl.ds(0, 2), pl.ds(2, 2)

    def aux_start(stage):
        axis = ("x", "y", "z")[stage]
        return [
            links.start(aux, aux_in.at[stage * 3 + d - 1], ring(at, axis, d)) for d in (1, 2, 3)
        ]

    def aux_add(stage, copies):
        for copy in copies:
            copy.wait()
            links.drop(copy)
        add_into(aux, *[aux_in.at[stage * 3 + d - 1] for d in (1, 2, 3)])

    def first_sends(view, opp, near, axis):
        me = at[axis]
        right, left = ring(at, axis, 1), ring(at, axis, 3)
        far = (me + 2) % 4
        a = links.start(view(far, high_half), opp.at[0], right)
        b = links.start(view(far, low), opp.at[1], left)
        c = links.start(view((me + 1) % 4, low), near.at[0, low], right)
        d = links.start(view((me + 3) % 4, high_half), near.at[1, high_half], left)
        return [a, b, c, d]

    def second_sends(view, opp, near, axis, copies):
        me = at[axis]
        right, left = ring(at, axis, 1), ring(at, axis, 3)
        copies[0].wait_recv()
        add_into(view((me + 1) % 4, high_half), opp.at[0])
        copies.append(links.start(view((me + 1) % 4, high_half), near.at[0, high_half], right))
        copies[1].wait_recv()
        add_into(view((me + 3) % 4, low), opp.at[1])
        copies.append(links.start(view((me + 3) % 4, low), near.at[1, low], left))

    def finish(view, near, axis, copies):
        for copy in copies[2:]:
            copy.wait_recv()
        add_into(view(at[axis], pl.ds(0, 4)), near.at[0], near.at[1])

    def view1(third):
        axis = ORDERS[third][0]
        halved = "x" if axis == "z" else "z"
        return lambda i, h: part(own, third, **{axis: i, halved: h})

    def view2(third):
        a, b, c = ORDERS[third]
        return lambda i, h: part(own, third, **{a: at[a], b: i, c: h})

    small = aux_start(0)
    one = [first_sends(view1(t), opp1.at[t], near1.at[t], ORDERS[t][0]) for t in range(3)]
    for t in range(3):
        second_sends(view1(t), opp1.at[t], near1.at[t], ORDERS[t][0], one[t])
    aux_add(0, small)
    small = aux_start(1)
    two = []
    for t in range(3):
        finish(view1(t), near1.at[t], ORDERS[t][0], one[t])
        two.append(first_sends(view2(t), opp2.at[t], near2.at[t], ORDERS[t][1]))
    for t in range(3):
        second_sends(view2(t), opp2.at[t], near2.at[t], ORDERS[t][1], two[t])
    aux_add(1, small)
    small = aux_start(2)
    three = []
    for t in range(3):
        finish(view2(t), near2.at[t], ORDERS[t][1], two[t])
        a, b, c = ORDERS[t]
        three.append(
            [
                links.start(
                    part(own, t, **{a: at[a], b: at[b], c: (at[c] + d) % 4}),
                    last3.at[t, d - 1],
                    ring(at, c, d),
                )
                for d in (1, 2, 3)
            ]
        )
    for t in range(3):
        total = part(own, t, z=at["z"], x=at["x"], y=at["y"])[...].astype(F32)
        for d in (1, 2, 3):
            three[t][d - 1].wait_recv()
            total = total + last3[t, d - 1].astype(F32)
        final[pl.ds(t * 16, 16)] = total
    swap = links.start(final.at[pl.ds(pl.multiple_of((1 - core) * 24, 8), 24)], final_in, sibling)
    gw_ref[:, my_cols] = final[pl.ds(pl.multiple_of(core * 24, 8), 24)]

    aux_add(2, small)
    aux_out_ref[...] = aux[...]
    swap.wait_recv()
    gw_ref[:, other_cols] = final_in[...]
    lax.fori_loop(0, 12, lambda j, carry: (core_copy(j).wait_send(), carry)[1], 0)
    links.drain()


def score_reduce(query, cand, hidden_weight, hidden_bias, score_weight, score_grad):
    vmem = pl.BlockSpec(memory_space=pltpu.VMEM)
    return pl.pallas_call(
        score_kernel,
        out_shape=(
            jax.ShapeDtypeStruct((64, 16), F32),
            jax.ShapeDtypeStruct((24, 1024), F32),
            jax.ShapeDtypeStruct((2, 1024), F32),
        ),
        in_specs=[vmem] * 6,
        out_specs=(vmem, vmem, vmem),
        scratch_shapes=[
            pltpu.VMEM((128, 1024), BF16),
            pltpu.VMEM((128, 1024), BF16),
            pltpu.VMEM((1024, 1024), BF16),
            pltpu.VMEM((1024, 1024), BF16),
            pltpu.VMEM((64, 1024), F32),
            pltpu.VMEM((8, 1024), F32),
            pltpu.VMEM((8, 1024), F32),
            pltpu.VMEM((4, 4, 4, 3, 16, 512), BF16),
            pltpu.VMEM((192, 16, 512), BF16),
            pltpu.VMEM((192, 16, 512), BF16),
            pltpu.VMEM((3, 2, 2, 4, 16, 512), BF16),
            pltpu.VMEM((3, 2, 4, 4, 16, 512), BF16),
            pltpu.VMEM((3, 2, 2, 16, 512), BF16),
            pltpu.VMEM((3, 2, 4, 16, 512), BF16),
            pltpu.VMEM((3, 3, 16, 512), BF16),
            pltpu.VMEM((48, 512), F32),
            pltpu.VMEM((24, 512), F32),
            pltpu.VMEM((2, 1024), F32),
            pltpu.VMEM((2, 1024), F32),
            pltpu.VMEM((9, 2, 1024), F32),
            pltpu.SemaphoreType.DMA((12,)),
            pltpu.SemaphoreType.DMA((12,)),
            pltpu.SemaphoreType.DMA((64,)),
            pltpu.SemaphoreType.DMA((64,)),
        ],
        compiler_params=pltpu.CompilerParams(
            collective_id=0, has_side_effects=True, vmem_limit_bytes=48 * 2**20
        ),
        cost_estimate=pl.CostEstimate(flops=13 * 10**9, bytes_accessed=12 * 10**6, transcendentals=10**6),
        name="score_reduce",
    )(
        query,
        cand,
        hidden_weight,
        hidden_bias.reshape(1, 1024),
        score_weight.astype(F32).reshape(1, 1024),
        score_grad,
    )


def body(
    node_feats,
    msg_weight,
    msg_bias,
    edge_source,
    edge_slot,
    edge_target,
    edge_weight,
    update_weight,
    update_bias,
    pair_ids,
    neg_ids,
    hidden_weight,
    hidden_bias,
    score_weight,
    score_grad,
):
    node_count = lax.axis_size("node")
    node_dev, feature_dim = node_feats.shape
    edges_dev = edge_source.shape[0]
    slot_count = max(2, 2 * edges_dev // node_count)
    project = jax.nn.relu(
        jnp.dot(node_feats, msg_weight, preferred_element_type=jnp.float32) + msg_bias
    )
    weight_f = edge_weight.astype(jnp.float32)
    message = (weight_f[:, None] * project[edge_source]).astype(jnp.bfloat16)
    slot_total = node_count * slot_count
    buffer = jnp.zeros((slot_total, feature_dim), jnp.bfloat16).at[edge_slot].set(message)
    weight_slots = jnp.zeros((slot_total,), jnp.bfloat16).at[edge_slot].set(edge_weight)
    target_slots = jnp.zeros((slot_total,), jnp.int32).at[edge_slot].set(edge_target)
    got_rows, got_weights, got_targets = (
        lax.all_to_all(
            buffer.reshape(node_count, slot_count, feature_dim),
            "node",
            split_axis=0,
            concat_axis=0,
            tiled=True,
        ),
        lax.all_to_all(
            weight_slots.reshape(node_count, slot_count),
            "node",
            split_axis=0,
            concat_axis=0,
            tiled=True,
        ),
        lax.all_to_all(
            target_slots.reshape(node_count, slot_count),
            "node",
            split_axis=0,
            concat_axis=0,
            tiled=True,
        ),
    )
    onehot = (
        got_targets.reshape(-1)[None, :] == jnp.arange(node_dev, dtype=jnp.int32)[:, None]
    ).astype(jnp.bfloat16)
    sums = jnp.dot(onehot, got_rows.reshape(-1, feature_dim), preferred_element_type=jnp.float32)
    totals = jnp.dot(onehot, got_weights.reshape(-1), preferred_element_type=jnp.float32)
    average = (sums / jnp.maximum(totals, 1.0)[:, None]).astype(jnp.bfloat16)
    joined = jnp.concatenate([node_feats, average], axis=1)
    rectified = jax.nn.relu(
        jnp.dot(joined, update_weight, preferred_element_type=jnp.float32) + update_bias
    )
    embedding = (
        rectified * lax.rsqrt(jnp.mean(rectified * rectified, axis=-1, keepdims=True) + 1e-06)
    ).astype(jnp.bfloat16)
    cand_ids = jnp.concatenate([pair_ids[:, 1:2], neg_ids], axis=1).T.reshape(-1)
    ask_ids = jnp.concatenate([pair_ids[:, 0], cand_ids])
    shard_rows = lax.all_gather(embedding, "node", axis=0, tiled=True)
    onehot = (ask_ids[:, None] == jnp.arange(shard_rows.shape[0], dtype=jnp.int32)[None, :]).astype(
        jnp.bfloat16
    )
    fetched = jnp.dot(onehot, shard_rows, preferred_element_type=jnp.float32).astype(jnp.bfloat16)
    scores, shared_weight, aux = score_reduce(
        fetched[:64], fetched[64:], hidden_weight, hidden_bias, score_weight, score_grad
    )
    index = lax.axis_index("pair") * 32 + lax.axis_index("node")
    mine = lax.dynamic_slice(aux, (0, index * 8), (2, 8))
    shared_bias, shared_score = mine[0], mine[1]
    return (embedding, scores, shared_weight, shared_bias, shared_score)


def solution(mesh):
    return jax.shard_map(
        body,
        mesh=mesh,
        in_specs=(
            P("node", None),
            P(),
            P(),
            P("node"),
            P("node"),
            P("node"),
            P("node"),
            P(),
            P(),
            P(("pair", "node"), None),
            P(("pair", "node"), None),
            P(),
            P(),
            P(),
            P(("pair", "node"), None),
        ),
        out_specs=(
            P("node", None),
            P(("pair", "node"), None),
            P(("pair", "node"), None),
            P(("pair", "node")),
            P(("pair", "node")),
        ),
        check_vma=False,
    )
```

```python
import functools
import jax
import jax.numpy as jnp
from jax import lax
from jax.experimental import pallas as pl
from jax.experimental.pallas import tpu as pltpu
from jax.sharding import PartitionSpec as P

MESH = pl.DeviceIdType.MESH
F32 = jnp.float32
BF16 = jnp.bfloat16
ORDERS = (("z", "x", "y"), ("x", "y", "z"), ("y", "z", "x"))


def place():
    node = lax.axis_index("node")
    return {
        "z": lax.axis_index("pair"),
        "x": node // 8,
        "y": (node // 2) % 4,
        "c": node % 2,
    }


def device(at, **other):
    pos = dict(at, **other)
    return (pos["z"], pos["x"] * 8 + pos["y"] * 2 + pos["c"])


def ring(at, axis, step):
    return device(at, **{axis: (at[axis] + step) % 4})


def part(ref, third, **sel):
    full = pl.ds(0, 4)
    return ref.at[sel.get("z", full), sel.get("x", full), sel.get("y", full), third]


def spot(n):
    chip = n // 3
    return (chip // 16, (chip // 4) % 4, chip % 4, n % 3)


class Links:
    def __init__(self, send_sem, recv_sem):
        self.send_sem, self.recv_sem, self.count, self.copies = send_sem, recv_sem, 0, []

    def start(self, src, dst, to):
        copy = pltpu.make_async_remote_copy(
            src_ref=src,
            dst_ref=dst,
            send_sem=self.send_sem.at[self.count],
            recv_sem=self.recv_sem.at[self.count],
            device_id=to,
            device_id_type=MESH,
        )
        copy.start()
        self.count += 1
        self.copies.append(copy)
        return copy

    def drop(self, done):
        self.copies = [copy for copy in self.copies if copy is not done]

    def drain(self):
        for copy in self.copies:
            copy.wait_send()


def add_into(dst, *srcs):
    total = dst[...].astype(F32)
    for src in srcs:
        total = total + src[...].astype(F32)
    dst[...] = total.astype(dst.dtype)


GATHER_UNITS = ((0, 5), (5, 5), (10, 6))


def table(ref, half, units, **sel):
    full = pl.ds(0, 4)
    return ref.at[sel.get("z", full), sel.get("x", full), sel.get("y", full), half, pl.ds(*units)]


def network_kernel(
    feats_ref, mw_hbm, mb_ref, source_ref, slot_ref, target_ref, weight_ref,
    uw_hbm, ub_ref, pair_ref, neg_ref, hw_hbm, hb_ref, sw_ref, sg_ref,
    emb_ref, scores_ref, gw_ref, aux_out_ref,
    mw, uw, hw_ref, outbox, inbox, avg_out, avg_in, rows_f, shared, keys, onehot, acc, q_ref, cand_ref,
    q2, gq2, prod, grad, query_act, acc_bias, acc_score,
    own, give, take,
    opp1, near1, opp2, near2, last3, final, final_in,
    aux, aux_core, aux_in,
    load_sem, msg_send, msg_recv, core_send, core_recv, send_sem, recv_sem,
):
    at = place()
    core = at["c"]
    node = lax.axis_index("node")
    sibling = device(at, c=1 - core)
    barrier = pltpu.get_barrier_semaphore()

    def greet(k, carry):
        pl.semaphore_signal(
            barrier, inc=1, device_id=(at["z"], (node + k) % 32), device_id_type=MESH
        )
        return carry

    lax.fori_loop(1, 32, greet, 0)
    for step in (1, 2, 3):
        pl.semaphore_signal(barrier, inc=1, device_id=ring(at, "z", step), device_id_type=MESH)
    links = Links(send_sem, recv_sem)

    quarter = pl.ds(pl.multiple_of(at["z"] * 256, 256), 256)
    load_mw = pltpu.make_async_copy(mw_hbm.at[:, quarter], mw, load_sem.at[0])
    load_uw = pltpu.make_async_copy(uw_hbm, uw, load_sem.at[1])
    load_hw = pltpu.make_async_copy(hw_hbm, hw_ref, load_sem.at[2])
    load_mw.start()
    load_uw.start()
    load_hw.start()

    def pick(cond):
        return jnp.where(cond, 1.0, 0.0).astype(BF16)

    row = lax.broadcasted_iota(jnp.int32, (128, 256), 0)
    weight = weight_ref[...]
    target = target_ref[...].astype(F32)
    from_node = jnp.where(row == source_ref[...], weight, 0.0)
    beside = jnp.where(row == 0, weight, jnp.where(row == 1, target, 0.0))
    edge_rows = jnp.concatenate([from_node, beside], axis=0).astype(BF16)
    to_slot = pick(lax.broadcasted_iota(jnp.int32, (512, 256), 0) == slot_ref[...])
    routed = lax.dot_general(
        to_slot, edge_rows, (((1,), (1,)), ((), ())), preferred_element_type=F32
    ).astype(BF16)
    load_mw.wait()
    project = jnp.dot(feats_ref[...], mw[...], preferred_element_type=F32) + mb_ref[:, quarter]
    project = jnp.maximum(project, 0.0).astype(BF16)
    message = jnp.dot(routed[:, :128], project, preferred_element_type=F32).astype(BF16)
    outbox[:, :, pl.ds(0, 256)] = message.reshape(32, 16, 256)
    outbox[:, :, pl.ds(256, 128)] = routed[:, 128:].reshape(32, 16, 128)
    pl.semaphore_wait(barrier, 34)

    def message_copy(k):
        to = (node + k) % 32
        return pltpu.make_async_remote_copy(
            src_ref=outbox.at[to],
            dst_ref=inbox.at[node],
            send_sem=msg_send.at[k],
            recv_sem=msg_recv.at[k],
            device_id=(at["z"], to),
            device_id_type=MESH,
        )

    def send_message(k, carry):
        message_copy(k).start()
        return carry

    def wait_message(k, carry):
        message_copy(k).wait_recv()
        return carry

    lax.fori_loop(1, 32, send_message, 0)
    inbox[node] = outbox[node]
    my_rows = pl.ds(pl.multiple_of(at["z"] * 32, 32), 32)
    load_uw.wait()
    rows_f[...] = (
        jnp.dot(feats_ref[my_rows], uw[pl.ds(0, 1024)], preferred_element_type=F32) + ub_ref[...]
    )
    ids = [pair_ref[:, 0:1], pair_ref[:, 1:2]] + [neg_ref[:, k : k + 1] for k in range(15)]
    for k, column in enumerate(ids):
        key = (
            ((column >> 5) & 3) * 1024 + ((column >> 7) & 1) * 512 + (column >> 8) * 32 + (column & 31)
        )
        keys[pl.ds(k * 64, 64)] = jnp.broadcast_to(key, (64, 128))
    lax.fori_loop(1, 32, wait_message, 0)

    got = inbox[...].reshape(512, 384)
    got_target = got[:, 256:].astype(F32)[:, 1:2]
    lane = lax.broadcasted_iota(jnp.int32, (512, 128), 1).astype(F32)
    to_row = pick(got_target == lane)
    sums = lax.dot_general(to_row, got, (((0,), (0,)), ((), ())), preferred_element_type=F32)
    average = (sums[:, :256] / jnp.maximum(sums[:, 256:257], 1.0)).astype(BF16)
    avg_out[...] = average.reshape(4, 32, 256)
    copies = [
        links.start(avg_out.at[(at["z"] + d) % 4], avg_in.at[at["z"]], ring(at, "z", d))
        for d in (1, 2, 3)
    ]
    avg_in[at["z"]] = avg_out[at["z"]]
    for copy in copies:
        copy.wait_recv()
    rect = rows_f[...]
    for k in range(4):
        rect = rect + jnp.dot(
            avg_in[k], uw[pl.ds(1024 + k * 256, 256)], preferred_element_type=F32
        )
    rect = jnp.maximum(rect, 0.0)
    scale = lax.rsqrt(jnp.mean(rect * rect, axis=1, keepdims=True) + 1e-06)
    emb = (rect * scale).astype(BF16)

    chip = {"z": at["z"], "x": at["x"], "y": at["y"]}
    for half in range(2):
        for t in range(4):
            for h in range(2):
                shared[at["z"], at["x"], at["y"], half, core * 8 + t * 2 + h] = emb[
                    h * 16 : (h + 1) * 16, half * 512 + t * 128 : half * 512 + (t + 1) * 128
                ]
    mine_units = (core * 8, 8)
    crossing = table(shared, 1 - core, mine_units, **chip)
    keeping = table(shared, core, mine_units, **chip)
    arrivals = [links.start(crossing, crossing, sibling)]
    arrivals.append(links.start(keeping, keeping, sibling))
    arrivals[0].wait_recv()

    def pass_on(view, to):
        return links.start(view, view, to)

    low, high = pl.ds(0, 2), pl.ds(2, 2)
    held = lambda p, **sel: table(shared, core, GATHER_UNITS[p], **sel)
    first = []
    for p in range(3):
        a = ORDERS[p][0]
        first.append([pass_on(held(p, **chip), ring(at, a, d)) for d in (1, 2, 3)])

    def both_ways(p, axis, **sel):
        view = held(p, **sel, **{axis: at[axis]})
        return [pass_on(view, ring(at, axis, 1)), pass_on(view, ring(at, axis, 3))]

    def forward_halves(p, axis, halved, copies, **sel):
        me = at[axis]
        copies[0].wait_recv()
        left = {axis: (me + 3) % 4}
        copies.append(pass_on(held(p, **sel, **left, **{halved: low}), ring(at, axis, 1)))
        arrivals.append(pass_on(held(p, **sel, **left), sibling))
        copies[1].wait_recv()
        right = {axis: (me + 1) % 4}
        copies.append(pass_on(held(p, **sel, **right, **{halved: high}), ring(at, axis, 3)))
        arrivals.append(pass_on(held(p, **sel, **right), sibling))

    def last_halves(p, axis, copies, **sel):
        copies[2].wait_recv()
        copies[3].wait_recv()

    def far_view(p, axis, **sel):
        return held(p, **sel, **{axis: (at[axis] + 2) % 4})

    second = []
    for p in range(3):
        a, b, c = ORDERS[p]
        for d in (1, 2, 3):
            first[p][d - 1].wait_recv()
        second.append(both_ways(p, b, **{c: at[c]}))
        for d in (1, 2, 3):
            arrivals.append(
                pass_on(held(p, **{a: (at[a] + d) % 4, b: at[b], c: at[c]}), sibling)
            )
    for p in range(3):
        a, b, c = ORDERS[p]
        forward_halves(p, b, a, second[p], **{c: at[c]})
    third = []
    for p in range(3):
        a, b, c = ORDERS[p]
        last_halves(p, b, second[p])
        third.append(both_ways(p, c))
        arrivals.append(pass_on(far_view(p, b, **{c: at[c]}), sibling))
    for p in range(3):
        a, b, c = ORDERS[p]
        forward_halves(p, c, a, third[p])
    for p in range(3):
        a, b, c = ORDERS[p]
        last_halves(p, c, third[p])
        arrivals.append(pass_on(far_view(p, c), sibling))
    for copy in arrivals[1:]:
        copy.wait_recv()

    for z in range(4):
        for half in range(2):
            for t in range(4):
                emb_ref[pl.ds(z * 32, 32), pl.ds(half * 512 + t * 128, 128)] = shared[
                    z, at["x"], at["y"], half, pl.ds(core * 8 + t * 2, 2)
                ].reshape(32, 128)

    acc[...] = jnp.zeros_like(acc)

    def fetch(z, carry):
        tile_lane = lax.broadcasted_iota(jnp.int32, (1088, 128), 1) + z * 1024
        for k in range(8):
            onehot[:, pl.ds(k * 128, 128)] = pick(keys[...] == tile_lane + k * 128)
        for half in range(2):
            for pair in range(2):
                tiles = []
                for t in (2 * pair, 2 * pair + 1):
                    tiles.append(
                        jnp.concatenate(
                            [
                                shared[z, :, :, half, pl.ds(s * 8 + t * 2, 2)].reshape(512, 128)
                                for s in (0, 1)
                            ],
                            axis=0,
                        )
                    )
                cols = pl.ds(half * 512 + pair * 256, 256)
                acc[:, cols] = acc[:, cols] + jnp.dot(
                    onehot[...], jnp.concatenate(tiles, axis=1), preferred_element_type=F32
                )
        return carry

    lax.fori_loop(0, 4, fetch, 0)
    q_ref[...] = acc[pl.ds(0, 64)].astype(BF16)
    cand_ref[...] = acc[pl.ds(64, 1024)].astype(BF16)
    load_hw.wait()

    query = q_ref[...]
    q2[pl.ds(0, 64)] = query
    q2[pl.ds(64, 64)] = query
    query_act[...] = jnp.dot(query, hw_ref[pl.ds(0, 1024)], preferred_element_type=F32) + hb_ref[...]
    acc_bias[...] = jnp.zeros_like(acc_bias)
    acc_score[...] = jnp.zeros_like(acc_score)
    scores_ref[...] = jnp.zeros_like(scores_ref)

    def forward(i, query_grad):
        rows = pl.ds(pl.multiple_of(i * 256, 256), 256)
        cand = cand_ref[rows]
        query = q_ref[...]
        product = (cand.astype(F32).reshape(4, 64, 1024) * query.astype(F32)[None]).astype(BF16).reshape(256, 1024)
        prod[rows] = product
        act = jnp.dot(cand, hw_ref[pl.ds(1024, 1024)], preferred_element_type=F32)
        act = act + jnp.dot(product, hw_ref[pl.ds(2048, 1024)], preferred_element_type=F32)
        sw = sw_ref[...].astype(F32)
        sg = sg_ref[...]
        lane = lax.broadcasted_iota(jnp.int32, (64, 16), 1)
        score = scores_ref[...]
        bias_sum = acc_bias[...]
        score_sum = acc_score[...]
        for k in range(4):
            mine = lane == i * 4 + k
            x = act[k * 64 : (k + 1) * 64] + query_act[...]
            s = 0.5 * jnp.tanh(0.5 * x) + 0.5
            hidden = (x * s).astype(BF16).astype(F32)
            score = score + jnp.where(mine, jnp.sum(hidden * sw, axis=1, keepdims=True), 0.0)
            cot = jnp.sum(jnp.where(mine, sg, 0.0), axis=1, keepdims=True)
            score_sum = score_sum + jnp.sum((cot * hidden).reshape(8, 8, 1024), axis=0)
            pre_grad = (cot * sw * s * (1.0 + x * (1.0 - s))).astype(BF16)
            grad[pl.ds(pl.multiple_of(i * 256 + k * 64, 64), 64)] = pre_grad
            pre_grad = pre_grad.astype(F32)
            bias_sum = bias_sum + jnp.sum(pre_grad.reshape(8, 8, 1024), axis=0)
            query_grad = query_grad + pre_grad
        scores_ref[...] = score
        acc_bias[...] = bias_sum
        acc_score[...] = score_sum
        return query_grad

    query_grad = lax.fori_loop(0, 4, forward, jnp.zeros((64, 1024), F32))
    high = query_grad.astype(BF16)
    gq2[pl.ds(0, 64)] = high
    gq2[pl.ds(64, 64)] = (query_grad - high.astype(F32)).astype(BF16)
    aux[pl.ds(0, 1)] = jnp.sum(acc_bias[...], axis=0, keepdims=True)
    aux[pl.ds(1, 1)] = jnp.sum(acc_score[...], axis=0, keepdims=True)
    aux_core_copy = links.start(aux, aux_core, sibling)

    def core_copy(j):
        blocks = pl.ds(j * 16, 16)
        return pltpu.make_async_remote_copy(
            src_ref=give.at[blocks],
            dst_ref=take.at[blocks],
            send_sem=core_send.at[j],
            recv_sem=core_recv.at[j],
            device_id=sibling,
            device_id_type=MESH,
        )

    my_cols = pl.ds(pl.multiple_of(core * 512, 512), 512)
    other_cols = pl.ds(pl.multiple_of((1 - core) * 512, 512), 512)
    contract = (((0,), (0,)), ((), ()))

    def chunk(j, x_ref, g_ref, k):
        x = x_ref[:, pl.ds(pl.multiple_of(k * 256, 256), 256)]
        other = lax.dot_general(x, g_ref[:, other_cols], contract, preferred_element_type=F32)
        give[pl.ds(j * 16, 16)] = other.astype(BF16).reshape(16, 16, 512)
        core_copy(j).start()
        mine = lax.dot_general(x, g_ref[:, my_cols], contract, preferred_element_type=F32)
        mine = mine.astype(BF16)
        for b in range(16):
            own[spot(j * 16 + b)] = mine[b * 16 : (b + 1) * 16]

    def land(j):
        core_copy(j).wait_recv()
        for b in range(16):
            n = j * 16 + b
            own[spot(n)] = (own[spot(n)].astype(F32) + take[n].astype(F32)).astype(BF16)

    def weight_c(k, carry):
        chunk(k + 4, cand_ref, grad, k)
        return carry

    def weight_p(k, carry):
        chunk(k + 8, prod, grad, k)
        land(k + 4)
        return carry

    def weight_q(k, carry):
        chunk(k, q2, gq2, k)
        land(k + 8)
        return carry

    def weight_last(k, carry):
        land(k)
        return carry

    lax.fori_loop(0, 4, weight_c, 0)
    lax.fori_loop(0, 4, weight_p, 0)
    lax.fori_loop(0, 4, weight_q, 0)
    aux_core_copy.wait()
    links.drop(aux_core_copy)
    add_into(aux, aux_core)
    lax.fori_loop(0, 4, weight_last, 0)

    low, high_half = pl.ds(0, 2), pl.ds(2, 2)

    def aux_start(stage):
        axis = ("x", "y", "z")[stage]
        return [
            links.start(aux, aux_in.at[stage * 3 + d - 1], ring(at, axis, d)) for d in (1, 2, 3)
        ]

    def aux_add(stage, copies):
        for copy in copies:
            copy.wait()
            links.drop(copy)
        add_into(aux, *[aux_in.at[stage * 3 + d - 1] for d in (1, 2, 3)])

    def first_sends(view, opp, near, axis):
        me = at[axis]
        right, left = ring(at, axis, 1), ring(at, axis, 3)
        far = (me + 2) % 4
        a = links.start(view(far, high_half), opp.at[0], right)
        b = links.start(view(far, low), opp.at[1], left)
        c = links.start(view((me + 1) % 4, low), near.at[0, low], right)
        d = links.start(view((me + 3) % 4, high_half), near.at[1, high_half], left)
        return [a, b, c, d]

    def second_sends(view, opp, near, axis, copies):
        me = at[axis]
        right, left = ring(at, axis, 1), ring(at, axis, 3)
        copies[0].wait_recv()
        add_into(view((me + 1) % 4, high_half), opp.at[0])
        copies.append(links.start(view((me + 1) % 4, high_half), near.at[0, high_half], right))
        copies[1].wait_recv()
        add_into(view((me + 3) % 4, low), opp.at[1])
        copies.append(links.start(view((me + 3) % 4, low), near.at[1, low], left))

    def finish(view, near, axis, copies):
        for copy in copies[2:]:
            copy.wait_recv()
        add_into(view(at[axis], pl.ds(0, 4)), near.at[0], near.at[1])

    def view1(third):
        axis = ORDERS[third][0]
        halved = "x" if axis == "z" else "z"
        return lambda i, h: part(own, third, **{axis: i, halved: h})

    def view2(third):
        a, b, c = ORDERS[third]
        return lambda i, h: part(own, third, **{a: at[a], b: i, c: h})

    small = aux_start(0)
    one = [first_sends(view1(t), opp1.at[t], near1.at[t], ORDERS[t][0]) for t in range(3)]
    for t in range(3):
        second_sends(view1(t), opp1.at[t], near1.at[t], ORDERS[t][0], one[t])
    aux_add(0, small)
    small = aux_start(1)
    two = []
    for t in range(3):
        finish(view1(t), near1.at[t], ORDERS[t][0], one[t])
        two.append(first_sends(view2(t), opp2.at[t], near2.at[t], ORDERS[t][1]))
    for t in range(3):
        second_sends(view2(t), opp2.at[t], near2.at[t], ORDERS[t][1], two[t])
    aux_add(1, small)
    small = aux_start(2)
    three = []
    for t in range(3):
        finish(view2(t), near2.at[t], ORDERS[t][1], two[t])
        a, b, c = ORDERS[t]
        three.append(
            [
                links.start(
                    part(own, t, **{a: at[a], b: at[b], c: (at[c] + d) % 4}),
                    last3.at[t, d - 1],
                    ring(at, c, d),
                )
                for d in (1, 2, 3)
            ]
        )
    for t in range(3):
        total = part(own, t, z=at["z"], x=at["x"], y=at["y"])[...].astype(F32)
        for d in (1, 2, 3):
            three[t][d - 1].wait_recv()
            total = total + last3[t, d - 1].astype(F32)
        final[pl.ds(t * 16, 16)] = total
    swap = links.start(final.at[pl.ds(pl.multiple_of((1 - core) * 24, 8), 24)], final_in, sibling)
    gw_ref[:, my_cols] = final[pl.ds(pl.multiple_of(core * 24, 8), 24)]

    aux_add(2, small)
    aux_out_ref[...] = aux[...]
    swap.wait_recv()
    gw_ref[:, other_cols] = final_in[...]
    lax.fori_loop(0, 12, lambda j, carry: (core_copy(j).wait_send(), carry)[1], 0)
    links.drain()
    lax.fori_loop(1, 32, lambda k, carry: (message_copy(k).wait_send(), carry)[1], 0)


def network(*args):
    vmem = pl.BlockSpec(memory_space=pltpu.VMEM)
    hbm = pl.BlockSpec(memory_space=pl.ANY)
    return pl.pallas_call(
        network_kernel,
        out_shape=(
            jax.ShapeDtypeStruct((128, 1024), BF16),
            jax.ShapeDtypeStruct((64, 16), F32),
            jax.ShapeDtypeStruct((24, 1024), F32),
            jax.ShapeDtypeStruct((2, 1024), F32),
        ),
        in_specs=[vmem, hbm] + [vmem] * 5 + [hbm] + [vmem] * 3 + [hbm] + [vmem] * 3,
        out_specs=(vmem,) * 4,
        scratch_shapes=[
            pltpu.VMEM((1024, 256), BF16),
            pltpu.VMEM((2048, 1024), BF16),
            pltpu.VMEM((3072, 1024), BF16),
            pltpu.VMEM((32, 16, 384), BF16),
            pltpu.VMEM((32, 16, 384), BF16),
            pltpu.VMEM((4, 32, 256), BF16),
            pltpu.VMEM((4, 32, 256), BF16),
            pltpu.VMEM((32, 1024), F32),
            pltpu.VMEM((4, 4, 4, 2, 16, 16, 128), BF16),
            pltpu.VMEM((1088, 128), jnp.int32),
            pltpu.VMEM((1088, 1024), BF16),
            pltpu.VMEM((1088, 1024), F32),
            pltpu.VMEM((64, 1024), BF16),
            pltpu.VMEM((1024, 1024), BF16),
            pltpu.VMEM((128, 1024), BF16),
            pltpu.VMEM((128, 1024), BF16),
            pltpu.VMEM((1024, 1024), BF16),
            pltpu.VMEM((1024, 1024), BF16),
            pltpu.VMEM((64, 1024), F32),
            pltpu.VMEM((8, 1024), F32),
            pltpu.VMEM((8, 1024), F32),
            pltpu.VMEM((4, 4, 4, 3, 16, 512), BF16),
            pltpu.VMEM((192, 16, 512), BF16),
            pltpu.VMEM((192, 16, 512), BF16),
            pltpu.VMEM((3, 2, 2, 4, 16, 512), BF16),
            pltpu.VMEM((3, 2, 4, 4, 16, 512), BF16),
            pltpu.VMEM((3, 2, 2, 16, 512), BF16),
            pltpu.VMEM((3, 2, 4, 16, 512), BF16),
            pltpu.VMEM((3, 3, 16, 512), BF16),
            pltpu.VMEM((48, 512), F32),
            pltpu.VMEM((24, 512), F32),
            pltpu.VMEM((2, 1024), F32),
            pltpu.VMEM((2, 1024), F32),
            pltpu.VMEM((9, 2, 1024), F32),
            pltpu.SemaphoreType.DMA((3,)),
            pltpu.SemaphoreType.DMA((32,)),
            pltpu.SemaphoreType.DMA((32,)),
            pltpu.SemaphoreType.DMA((12,)),
            pltpu.SemaphoreType.DMA((12,)),
            pltpu.SemaphoreType.DMA((128,)),
            pltpu.SemaphoreType.DMA((128,)),
        ],
        compiler_params=pltpu.CompilerParams(
            collective_id=0, has_side_effects=True, vmem_limit_bytes=60 * 2**20
        ),
        cost_estimate=pl.CostEstimate(flops=22 * 10**9, bytes_accessed=14 * 10**6, transcendentals=10**6),
        name="network",
    )(*args)


def body(
    node_feats,
    msg_weight,
    msg_bias,
    edge_source,
    edge_slot,
    edge_target,
    edge_weight,
    update_weight,
    update_bias,
    pair_ids,
    neg_ids,
    hidden_weight,
    hidden_bias,
    score_weight,
    score_grad,
):
    embedding, scores, shared_weight, aux = network(
        node_feats,
        msg_weight,
        msg_bias.reshape(1, 1024),
        edge_source.reshape(1, 256),
        edge_slot.reshape(1, 256),
        edge_target.reshape(1, 256),
        edge_weight.astype(F32).reshape(1, 256),
        update_weight,
        update_bias.reshape(1, 1024),
        pair_ids,
        neg_ids,
        hidden_weight,
        hidden_bias.reshape(1, 1024),
        score_weight.astype(F32).reshape(1, 1024),
        score_grad,
    )
    index = lax.axis_index("pair") * 32 + lax.axis_index("node")
    mine = lax.dynamic_slice(aux, (0, index * 8), (2, 8))
    return (embedding, scores, shared_weight, mine[0], mine[1])


def solution(mesh):
    return jax.shard_map(
        body,
        mesh=mesh,
        in_specs=(
            P("node", None),
            P(),
            P(),
            P("node"),
            P("node"),
            P("node"),
            P("node"),
            P(),
            P(),
            P(("pair", "node"), None),
            P(("pair", "node"), None),
            P(),
            P(),
            P(),
            P(("pair", "node"), None),
        ),
        out_specs=(
            P("node", None),
            P(("pair", "node"), None),
            P(("pair", "node"), None),
            P(("pair", "node")),
            P(("pair", "node")),
        ),
        check_vma=False,
    )
```

```python
import functools
import jax
import jax.numpy as jnp
from jax import lax
from jax.experimental import pallas as pl
from jax.experimental.pallas import tpu as pltpu
from jax.sharding import PartitionSpec as P

MESH = pl.DeviceIdType.MESH
F32 = jnp.float32
BF16 = jnp.bfloat16
ORDERS = (("z", "x", "y"), ("x", "y", "z"), ("y", "z", "x"))


def place():
    node = lax.axis_index("node")
    return {
        "z": lax.axis_index("pair"),
        "x": node // 8,
        "y": (node // 2) % 4,
        "c": node % 2,
    }


def device(at, **other):
    pos = dict(at, **other)
    return (pos["z"], pos["x"] * 8 + pos["y"] * 2 + pos["c"])


def ring(at, axis, step):
    return device(at, **{axis: (at[axis] + step) % 4})


def part(ref, third, **sel):
    full = pl.ds(0, 4)
    return ref.at[sel.get("z", full), sel.get("x", full), sel.get("y", full), third]


def spot(n):
    chip = n // 3
    return (chip // 16, (chip // 4) % 4, chip % 4, n % 3)


class Links:
    def __init__(self, send_sem, recv_sem):
        self.send_sem, self.recv_sem, self.copies = send_sem, recv_sem, []
        self.sent = self.received = 0

    def start(self, src, dst, to):
        copy = pltpu.make_async_remote_copy(
            src_ref=src,
            dst_ref=dst,
            send_sem=self.send_sem.at[self.sent],
            recv_sem=self.recv_sem.at[self.received],
            device_id=to,
            device_id_type=MESH,
        )
        copy.start()
        self.sent += 1
        self.received += 1
        self.copies.append(copy)
        return copy

    def drop(self, done):
        self.copies = [copy for copy in self.copies if copy is not done]

    def drain(self):
        for copy in self.copies:
            copy.wait_send()
        self.copies, self.sent = [], 0


def add_into(dst, *srcs):
    if len(srcs) == 1:
        dst[...] = dst[...] + srcs[0][...]
        return
    total = dst[...].astype(F32)
    for src in srcs:
        total = total + src[...].astype(F32)
    dst[...] = total.astype(dst.dtype)


GATHER_UNITS = ((0, 5), (5, 5), (10, 6))


def table(ref, half, units, **sel):
    full = pl.ds(0, 4)
    return ref.at[sel.get("z", full), sel.get("x", full), sel.get("y", full), half, pl.ds(*units)]


def network_kernel(
    feats_ref, mw_hbm, mb_ref, source_ref, slot_ref, target_ref, weights_ref,
    uw_hbm, ub_ref, pair_ref, neg_ref, hw_hbm, hb_ref, sg_in,
    emb_ref, scores_out, gw_ref, aux_out_ref,
    turn, sg_ref, scores_ref,
    mw, uw, hw_ref, outbox, inbox, avg_out, avg_in, rows_f, shared, keys, onehot, acc, q_ref, cand_ref,
    q2t, qt8, gq2, query_act, acc_bias, acc_score,
    own, give, take,
    opp1, near1, opp2, near2, last3, final, final_in,
    aux, aux_core, aux_in,
    load_sem, msg_send, msg_recv, core_send, core_recv, send_sem, recv_sem,
):
    at = place()
    core = at["c"]
    node = lax.axis_index("node")
    sibling = device(at, c=1 - core)
    barrier = pltpu.get_barrier_semaphore()

    def greet(k, carry):
        pl.semaphore_signal(
            barrier, inc=1, device_id=(at["z"], (node + k) % 32), device_id_type=MESH
        )
        return carry

    lax.fori_loop(1, 32, greet, 0)
    for step in (1, 2, 3):
        pl.semaphore_signal(barrier, inc=1, device_id=ring(at, "z", step), device_id_type=MESH)
    links = Links(send_sem, recv_sem)

    quarter = pl.ds(pl.multiple_of(at["z"] * 256, 256), 256)
    load_mw = pltpu.make_async_copy(mw_hbm.at[:, quarter], mw, load_sem.at[0])
    load_uw = pltpu.make_async_copy(uw_hbm, uw, load_sem.at[1])
    load_hw = pltpu.make_async_copy(hw_hbm, hw_ref, load_sem.at[2])
    load_mw.start()
    load_uw.start()
    load_hw.start()

    def pick(cond):
        return jnp.where(cond, 1.0, 0.0).astype(BF16)

    row = lax.broadcasted_iota(jnp.int32, (128, 256), 0)
    weight = weights_ref[:, pl.ds(1024, 256)]
    target = target_ref[...].astype(F32)
    from_node = jnp.where(row == source_ref[...], weight, 0.0)
    beside = jnp.where(row == 0, weight, jnp.where(row == 1, target, 0.0))
    edge_rows = jnp.concatenate([from_node, beside], axis=0).astype(BF16)
    to_slot = pick(lax.broadcasted_iota(jnp.int32, (512, 256), 0) == slot_ref[...])
    routed = lax.dot_general(
        to_slot, edge_rows, (((1,), (1,)), ((), ())), preferred_element_type=F32
    ).astype(BF16)
    load_mw.wait()
    project = jnp.dot(feats_ref[...], mw[...], preferred_element_type=F32) + mb_ref[:, quarter]
    project = jnp.maximum(project, 0.0).astype(BF16)
    message = jnp.dot(routed[:, :128], project, preferred_element_type=F32).astype(BF16)
    outbox[:, :, pl.ds(0, 256)] = message.reshape(32, 16, 256)
    outbox[:, :, pl.ds(256, 128)] = routed[:, 128:].reshape(32, 16, 128)
    pl.semaphore_wait(barrier, 34)

    def message_copy(k):
        to = (node + k) % 32
        return pltpu.make_async_remote_copy(
            src_ref=outbox.at[to],
            dst_ref=inbox.at[node],
            send_sem=msg_send.at[k],
            recv_sem=msg_recv.at[k],
            device_id=(at["z"], to),
            device_id_type=MESH,
        )

    def send_message(k, carry):
        message_copy(k).start()
        return carry

    def wait_message(k, carry):
        message_copy(k).wait_recv()
        return carry

    lax.fori_loop(1, 32, send_message, 0)
    inbox[node] = outbox[node]
    my_rows = pl.ds(pl.multiple_of(at["z"] * 32, 32), 32)
    load_uw.wait()
    rows_f[...] = (
        jnp.dot(feats_ref[my_rows], uw[pl.ds(0, 1024)], preferred_element_type=F32) + ub_ref[...]
    )
    turn[...] = jnp.zeros_like(turn)
    turn[pl.ds(0, 2), pl.ds(0, 64)] = pair_ref[...].astype(F32)
    turn[pl.ds(2, 15), pl.ds(0, 64)] = neg_ref[...].astype(F32)
    turn[pl.ds(32, 16), pl.ds(0, 64)] = sg_in[...]
    turned = turn[...].T[:64]
    sg_ref[...] = turned[:, 32:48]
    ids = turned[:, :17].astype(jnp.int32)
    for k in range(17):
        column = ids[:, k : k + 1]
        key = (
            ((column >> 5) & 3) * 1024 + ((column >> 7) & 1) * 512 + (column >> 8) * 32 + (column & 31)
        )
        keys[pl.ds(k * 64, 64)] = jnp.broadcast_to(key, (64, 128))
    lax.fori_loop(1, 32, wait_message, 0)

    got = inbox[...].reshape(512, 384)
    got_target = got[:, 256:].astype(F32)[:, 1:2]
    lane = lax.broadcasted_iota(jnp.int32, (512, 128), 1).astype(F32)
    to_row = pick(got_target == lane)
    sums = lax.dot_general(to_row, got, (((0,), (0,)), ((), ())), preferred_element_type=F32)
    average = (sums[:, :256] / jnp.maximum(sums[:, 256:257], 1.0)).astype(BF16)
    avg_out[...] = average.reshape(4, 32, 256)
    copies = [
        links.start(avg_out.at[(at["z"] + d) % 4], avg_in.at[at["z"]], ring(at, "z", d))
        for d in (1, 2, 3)
    ]
    avg_in[at["z"]] = avg_out[at["z"]]
    for copy in copies:
        copy.wait_recv()
    rect = rows_f[...]
    for k in range(4):
        rect = rect + jnp.dot(
            avg_in[k], uw[pl.ds(1024 + k * 256, 256)], preferred_element_type=F32
        )
    rect = jnp.maximum(rect, 0.0)
    scale = lax.rsqrt(jnp.mean(rect * rect, axis=1, keepdims=True) + 1e-06)
    emb = (rect * scale).astype(BF16)

    chip = {"z": at["z"], "x": at["x"], "y": at["y"]}
    for half in range(2):
        for t in range(4):
            for h in range(2):
                shared[at["z"], at["x"], at["y"], half, core * 8 + t * 2 + h] = emb[
                    h * 16 : (h + 1) * 16, half * 512 + t * 128 : half * 512 + (t + 1) * 128
                ]
    mine_units = (core * 8, 8)
    crossing = table(shared, 1 - core, mine_units, **chip)
    keeping = table(shared, core, mine_units, **chip)
    arrivals = [links.start(crossing, crossing, sibling)]
    arrivals.append(links.start(keeping, keeping, sibling))
    arrivals[0].wait_recv()

    def pass_on(view, to):
        return links.start(view, view, to)

    low, high = pl.ds(0, 2), pl.ds(2, 2)
    held = lambda p, **sel: table(shared, core, GATHER_UNITS[p], **sel)
    first = []
    for p in range(3):
        a = ORDERS[p][0]
        first.append([pass_on(held(p, **chip), ring(at, a, d)) for d in (1, 2, 3)])

    def both_ways(p, axis, **sel):
        view = held(p, **sel, **{axis: at[axis]})
        return [pass_on(view, ring(at, axis, 1)), pass_on(view, ring(at, axis, 3))]

    def forward_halves(p, axis, halved, copies, **sel):
        me = at[axis]
        copies[0].wait_recv()
        left = {axis: (me + 3) % 4}
        copies.append(pass_on(held(p, **sel, **left, **{halved: low}), ring(at, axis, 1)))
        arrivals.append(pass_on(held(p, **sel, **left), sibling))
        copies[1].wait_recv()
        right = {axis: (me + 1) % 4}
        copies.append(pass_on(held(p, **sel, **right, **{halved: high}), ring(at, axis, 3)))
        arrivals.append(pass_on(held(p, **sel, **right), sibling))

    def last_halves(p, axis, copies, **sel):
        copies[2].wait_recv()
        copies[3].wait_recv()

    def far_view(p, axis, **sel):
        return held(p, **sel, **{axis: (at[axis] + 2) % 4})

    second = []
    for p in range(3):
        a, b, c = ORDERS[p]
        for d in (1, 2, 3):
            first[p][d - 1].wait_recv()
        second.append(both_ways(p, b, **{c: at[c]}))
        for d in (1, 2, 3):
            arrivals.append(
                pass_on(held(p, **{a: (at[a] + d) % 4, b: at[b], c: at[c]}), sibling)
            )
    for p in range(3):
        a, b, c = ORDERS[p]
        forward_halves(p, b, a, second[p], **{c: at[c]})
    third = []
    for p in range(3):
        a, b, c = ORDERS[p]
        last_halves(p, b, second[p])
        third.append(both_ways(p, c))
        arrivals.append(pass_on(far_view(p, b, **{c: at[c]}), sibling))
    for p in range(3):
        a, b, c = ORDERS[p]
        forward_halves(p, c, a, third[p])
    for p in range(3):
        a, b, c = ORDERS[p]
        last_halves(p, c, third[p])
        arrivals.append(pass_on(far_view(p, c), sibling))
    for copy in arrivals[1:]:
        copy.wait_recv()

    for z in range(4):
        for half in range(2):
            for t in range(4):
                emb_ref[pl.ds(z * 32, 32), pl.ds(half * 512 + t * 128, 128)] = shared[
                    z, at["x"], at["y"], half, pl.ds(core * 8 + t * 2, 2)
                ].reshape(32, 128)

    acc[...] = jnp.zeros_like(acc)

    def fetch(z, carry):
        tile_lane = lax.broadcasted_iota(jnp.int32, (1088, 128), 1) + z * 1024
        for k in range(8):
            onehot[:, pl.ds(k * 128, 128)] = pick(keys[...] == tile_lane + k * 128)
        for half in range(2):
            for pair in range(2):
                tiles = []
                for t in (2 * pair, 2 * pair + 1):
                    tiles.append(
                        jnp.concatenate(
                            [
                                shared[z, :, :, half, pl.ds(s * 8 + t * 2, 2)].reshape(512, 128)
                                for s in (0, 1)
                            ],
                            axis=0,
                        )
                    )
                cols = pl.ds(half * 512 + pair * 256, 256)
                acc[:, cols] = acc[:, cols] + jnp.dot(
                    onehot[...], jnp.concatenate(tiles, axis=1), preferred_element_type=F32
                )
        return carry

    lax.fori_loop(0, 4, fetch, 0)
    q_ref[...] = acc[pl.ds(0, 64)].astype(BF16)
    cand_ref[...] = acc[pl.ds(64, 1024)].astype(BF16)
    load_hw.wait()

    links.drain()
    candt, prodt = uw.at[pl.ds(0, 1024)], uw.at[pl.ds(1024, 1024)]
    grad = onehot.at[pl.ds(0, 1024)]
    query_t = q_ref[...].T
    q2t[...] = jnp.concatenate([query_t, query_t], axis=1)
    qt8[...] = jnp.concatenate([query_t] * 8, axis=1)
    query_act[...] = jnp.dot(q_ref[...], hw_ref[pl.ds(0, 1024)], preferred_element_type=F32) + hb_ref[...]
    acc_bias[...] = jnp.zeros_like(acc_bias)
    acc_score[...] = jnp.zeros_like(acc_score)
    scores_ref[...] = jnp.zeros_like(scores_ref)

    def forward(i, query_grad):
        rows = pl.ds(pl.multiple_of(i * 512, 512), 512)
        cand = cand_ref[rows]
        product = (cand.reshape(8, 64, 1024) * q_ref[...][None]).reshape(512, 1024)
        act = jnp.dot(cand, hw_ref[pl.ds(1024, 1024)], preferred_element_type=F32)
        act = act + jnp.dot(product, hw_ref[pl.ds(2048, 1024)], preferred_element_type=F32)
        flipped = cand.T
        candt[:, rows] = flipped
        prodt[:, rows] = flipped * qt8[...]
        sw = weights_ref[:, pl.ds(0, 1024)]
        sg = sg_ref[...]
        lane = lax.broadcasted_iota(jnp.int32, (64, 16), 1)
        score = scores_ref[...]
        bias_sum = acc_bias[...]
        score_sum = acc_score[...]
        for k in range(8):
            mine = lane == i * 8 + k
            x = act[k * 64 : (k + 1) * 64] + query_act[...]
            s = 0.5 * jnp.tanh(0.5 * x) + 0.5
            hidden = (x * s).astype(BF16).astype(F32)
            score = score + jnp.where(mine, jnp.sum(hidden * sw, axis=1, keepdims=True), 0.0)
            cot = jnp.sum(jnp.where(mine, sg, 0.0), axis=1, keepdims=True)
            score_sum = score_sum + jnp.sum((cot * hidden).reshape(8, 8, 1024), axis=0)
            pre_grad = (cot * sw * s * (1.0 + x * (1.0 - s))).astype(BF16)
            grad[pl.ds(pl.multiple_of(i * 512 + k * 64, 64), 64)] = pre_grad
            pre_grad = pre_grad.astype(F32)
            bias_sum = bias_sum + jnp.sum(pre_grad.reshape(8, 8, 1024), axis=0)
            query_grad = query_grad + pre_grad
        scores_ref[...] = score
        acc_bias[...] = bias_sum
        acc_score[...] = score_sum
        return query_grad

    query_grad = lax.fori_loop(0, 2, forward, jnp.zeros((64, 1024), F32))
    high = query_grad.astype(BF16)
    gq2[pl.ds(0, 64)] = high
    gq2[pl.ds(64, 64)] = (query_grad - high.astype(F32)).astype(BF16)
    aux[pl.ds(0, 1)] = jnp.sum(acc_bias[...], axis=0, keepdims=True)
    aux[pl.ds(1, 1)] = jnp.sum(acc_score[...], axis=0, keepdims=True)
    aux_core_copy = links.start(aux, aux_core, sibling)

    def core_copy(n, j):
        return pltpu.make_async_remote_copy(
            src_ref=give.at[n, j],
            dst_ref=take.at[n, j],
            send_sem=core_send.at[n * 6 + j],
            recv_sem=core_recv.at[n * 6 + j],
            device_id=sibling,
            device_id_type=MESH,
        )

    def chunk(n, j, xt_ref, g_ref, k):
        x = xt_ref[pl.ds(pl.multiple_of(k * 512, 512), 512), :]
        cols = pl.ds(pl.multiple_of((1 - core) * 512 + n * 256, 256), 256)
        other = jnp.dot(x, g_ref[:, cols], preferred_element_type=F32)
        give[n, j] = other.astype(BF16).reshape(32, 16, 256)
        core_copy(n, j).start()
        cols = pl.ds(pl.multiple_of(core * 512 + n * 256, 256), 256)
        mine = jnp.dot(x, g_ref[:, cols], preferred_element_type=F32).astype(BF16)
        for b in range(32):
            own[(n,) + spot(j * 32 + b)] = mine[b * 16 : (b + 1) * 16]

    def land(n, j):
        core_copy(n, j).wait_recv()
        for b in range(32):
            to = (n,) + spot(j * 32 + b)
            own[to] = own[to] + take[n, j, b]

    def loop(body):
        for k in range(2):
            body(k)

    def step_c(n):
        def run(k):
            chunk(n, k + 2, candt, grad, k)
            if n == 1:
                land(0, k)

        loop(run)

    def step_p(n):
        def run(k):
            chunk(n, k + 4, prodt, grad, k)
            land(n, k + 2)

        loop(run)

    def step_q(n):
        def run(k):
            chunk(n, k, q2t, gq2, k)
            land(n, k + 4)

        loop(run)

    my_cols = pl.ds(pl.multiple_of(core * 512, 512), 512)
    other_cols = pl.ds(pl.multiple_of((1 - core) * 512, 512), 512)

    low, high_half = pl.ds(0, 2), pl.ds(2, 2)

    def aux_start(stage):
        axis = ("x", "y", "z")[stage]
        return [
            links.start(aux, aux_in.at[stage * 3 + d - 1], ring(at, axis, d)) for d in (1, 2, 3)
        ]

    def aux_add(stage, copies):
        for copy in copies:
            copy.wait()
            links.drop(copy)
        add_into(aux, *[aux_in.at[stage * 3 + d - 1] for d in (1, 2, 3)])

    def first_sends(view, opp, near, axis):
        me = at[axis]
        right, left = ring(at, axis, 1), ring(at, axis, 3)
        far = (me + 2) % 4
        a = links.start(view(far, high_half), opp.at[0], right)
        b = links.start(view(far, low), opp.at[1], left)
        c = links.start(view((me + 1) % 4, low), near.at[0, low], right)
        d = links.start(view((me + 3) % 4, high_half), near.at[1, high_half], left)
        return [a, b, c, d]

    def second_sends(view, opp, near, axis, copies):
        me = at[axis]
        right, left = ring(at, axis, 1), ring(at, axis, 3)
        copies[0].wait_recv()
        add_into(view((me + 1) % 4, high_half), opp.at[0])
        copies.append(links.start(view((me + 1) % 4, high_half), near.at[0, high_half], right))
        copies[1].wait_recv()
        add_into(view((me + 3) % 4, low), opp.at[1])
        copies.append(links.start(view((me + 3) % 4, low), near.at[1, low], left))

    def finish(view, near, axis, copies):
        for copy in copies[2:]:
            copy.wait_recv()
        add_into(view(at[axis], pl.ds(0, 4)), near.at[0], near.at[1])

    def view1(n, third):
        axis = ORDERS[third][0]
        halved = "x" if axis == "z" else "z"
        return lambda i, h: part(own.at[n], third, **{axis: i, halved: h})

    def view2(n, third):
        a, b, c = ORDERS[third]
        return lambda i, h: part(own.at[n], third, **{a: at[a], b: i, c: h})

    def stage1_first(n):
        return [first_sends(view1(n, t), opp1.at[n, t], near1.at[n, t], ORDERS[t][0]) for t in range(3)]

    def stage1_second(n, copies):
        for t in range(3):
            second_sends(view1(n, t), opp1.at[n, t], near1.at[n, t], ORDERS[t][0], copies[t])

    def stage2_first(n, copies):
        sent = []
        for t in range(3):
            finish(view1(n, t), near1.at[n, t], ORDERS[t][0], copies[t])
            sent.append(first_sends(view2(n, t), opp2.at[n, t], near2.at[n, t], ORDERS[t][1]))
        return sent

    def stage2_second(n, copies):
        for t in range(3):
            second_sends(view2(n, t), opp2.at[n, t], near2.at[n, t], ORDERS[t][1], copies[t])

    def stage3(n, copies):
        sent = []
        for t in range(3):
            finish(view2(n, t), near2.at[n, t], ORDERS[t][1], copies[t])
            a, b, c = ORDERS[t]
            sent.append(
                [
                    links.start(
                        part(own.at[n], t, **{a: at[a], b: at[b], c: (at[c] + d) % 4}),
                        last3.at[n, t, d - 1],
                        ring(at, c, d),
                    )
                    for d in (1, 2, 3)
                ]
            )
        return sent

    def total(n, copies):
        for t in range(3):
            value = part(own.at[n], t, z=at["z"], x=at["x"], y=at["y"])[...].astype(F32)
            for d in (1, 2, 3):
                copies[t][d - 1].wait_recv()
                value = value + last3[n, t, d - 1].astype(F32)
            final[pl.ds(t * 16, 16), pl.ds(n * 256, 256)] = value

    step_c(0)
    step_p(0)
    step_q(0)
    step_c(1)
    left_1 = stage1_first(0)
    aux_core_copy.wait()
    links.drop(aux_core_copy)
    add_into(aux, aux_core)
    small = aux_start(0)
    step_p(1)
    stage1_second(0, left_1)
    step_q(1)
    left_2 = stage2_first(0, left_1)
    loop(lambda k: land(1, k))
    right_1 = stage1_first(1)
    aux_add(0, small)
    small = aux_start(1)
    stage2_second(0, left_2)
    stage1_second(1, right_1)
    left_3 = stage3(0, left_2)
    right_2 = stage2_first(1, right_1)
    aux_add(1, small)
    small = aux_start(2)
    stage2_second(1, right_2)
    total(0, left_3)
    right_3 = stage3(1, right_2)
    total(1, right_3)
    swap = links.start(final.at[pl.ds(pl.multiple_of((1 - core) * 24, 8), 24)], final_in, sibling)
    gw_ref[:, my_cols] = final[pl.ds(pl.multiple_of(core * 24, 8), 24)]

    aux_add(2, small)
    index = at["z"] * 32 + node
    near = aux[:, pl.ds(pl.multiple_of(index // 16 * 128, 128), 128)]
    aux_out_ref[...] = pltpu.roll(near, (16 - index % 16) * 8 % 128, axis=1)
    turn[pl.ds(0, 64), pl.ds(0, 16)] = scores_ref[...]
    scores_out[...] = turn[...].T[:16, :64]
    swap.wait_recv()
    gw_ref[:, other_cols] = final_in[...]
    lax.fori_loop(0, 6, lambda j, carry: (core_copy(0, j).wait_send(), core_copy(1, j).wait_send(), carry)[2], 0)
    links.drain()
    lax.fori_loop(1, 32, lambda k, carry: (message_copy(k).wait_send(), carry)[1], 0)


def network(*args):
    vmem = pl.BlockSpec(memory_space=pltpu.VMEM)
    hbm = pl.BlockSpec(memory_space=pl.ANY)
    return pl.pallas_call(
        network_kernel,
        out_shape=(
            jax.ShapeDtypeStruct((128, 1024), BF16),
            jax.ShapeDtypeStruct((16, 64), F32),
            jax.ShapeDtypeStruct((24, 1024), F32),
            jax.ShapeDtypeStruct((2, 128), F32),
        ),
        in_specs=[vmem, hbm] + [vmem] * 5 + [hbm] + [vmem] * 3 + [hbm] + [vmem] * 2,
        out_specs=(vmem,) * 4,
        scratch_shapes=[
            pltpu.VMEM((128, 128), F32),
            pltpu.VMEM((64, 16), F32),
            pltpu.VMEM((64, 16), F32),
            pltpu.VMEM((1024, 256), BF16),
            pltpu.VMEM((2048, 1024), BF16),
            pltpu.VMEM((3072, 1024), BF16),
            pltpu.VMEM((32, 16, 384), BF16),
            pltpu.VMEM((32, 16, 384), BF16),
            pltpu.VMEM((4, 32, 256), BF16),
            pltpu.VMEM((4, 32, 256), BF16),
            pltpu.VMEM((32, 1024), F32),
            pltpu.VMEM((4, 4, 4, 2, 16, 16, 128), BF16),
            pltpu.VMEM((1088, 128), jnp.int32),
            pltpu.VMEM((1088, 1024), BF16),
            pltpu.VMEM((1088, 1024), F32),
            pltpu.VMEM((64, 1024), BF16),
            pltpu.VMEM((1024, 1024), BF16),
            pltpu.VMEM((1024, 128), BF16),
            pltpu.VMEM((1024, 512), BF16),
            pltpu.VMEM((128, 1024), BF16),
            pltpu.VMEM((64, 1024), F32),
            pltpu.VMEM((8, 1024), F32),
            pltpu.VMEM((8, 1024), F32),
            pltpu.VMEM((2, 4, 4, 4, 3, 16, 256), BF16),
            pltpu.VMEM((2, 6, 32, 16, 256), BF16),
            pltpu.VMEM((2, 6, 32, 16, 256), BF16),
            pltpu.VMEM((2, 3, 2, 2, 4, 16, 256), BF16),
            pltpu.VMEM((2, 3, 2, 4, 4, 16, 256), BF16),
            pltpu.VMEM((2, 3, 2, 2, 16, 256), BF16),
            pltpu.VMEM((2, 3, 2, 4, 16, 256), BF16),
            pltpu.VMEM((2, 3, 3, 16, 256), BF16),
            pltpu.VMEM((48, 512), F32),
            pltpu.VMEM((24, 512), F32),
            pltpu.VMEM((2, 1024), F32),
            pltpu.VMEM((2, 1024), F32),
            pltpu.VMEM((9, 2, 1024), F32),
            pltpu.SemaphoreType.DMA((3,)),
            pltpu.SemaphoreType.DMA((32,)),
            pltpu.SemaphoreType.DMA((32,)),
            pltpu.SemaphoreType.DMA((12,)),
            pltpu.SemaphoreType.DMA((12,)),
            pltpu.SemaphoreType.DMA((104,)),
            pltpu.SemaphoreType.DMA((176,)),
        ],
        compiler_params=pltpu.CompilerParams(
            collective_id=0, has_side_effects=True, vmem_limit_bytes=60 * 2**20
        ),
        cost_estimate=pl.CostEstimate(flops=22 * 10**9, bytes_accessed=14 * 10**6, transcendentals=10**6),
        name="network",
    )(*args)


def hand_over_kernel(emb, scores, weight, aux, emb_out, scores_out, weight_out, bias_out, score_out):
    emb_out[...] = emb[...]
    scores_out[...] = scores[...]
    weight_out[...] = weight[...]
    bias_out[...] = aux[0:1, 0:8]
    score_out[...] = aux[1:2, 0:8]


def hand_over(*arrays):
    vmem = pl.BlockSpec(memory_space=pltpu.VMEM)
    return pl.pallas_call(
        hand_over_kernel,
        out_shape=(
            jax.ShapeDtypeStruct((128, 1024), BF16),
            jax.ShapeDtypeStruct((16, 64), F32),
            jax.ShapeDtypeStruct((24, 1024), F32),
            jax.ShapeDtypeStruct((1, 8), F32),
            jax.ShapeDtypeStruct((1, 8), F32),
        ),
        in_specs=[vmem] * 4,
        out_specs=(vmem,) * 5,
        compiler_params=pltpu.CompilerParams(vmem_limit_bytes=60 * 2**20),
        name="hand_over",
    )(*arrays)


def body(
    node_feats,
    msg_weight,
    msg_bias,
    edge_source,
    edge_slot,
    edge_target,
    edge_weight,
    update_weight,
    update_bias,
    pair_ids,
    neg_ids,
    hidden_weight,
    hidden_bias,
    score_weight,
    score_grad,
):
    weights = lax.optimization_barrier(
        jnp.concatenate([score_weight.astype(F32), edge_weight.astype(F32)])
    )
    embedding, scores, shared_weight, aux = network(
        node_feats,
        msg_weight,
        msg_bias.reshape(1, 1024),
        edge_source.reshape(1, 256),
        edge_slot.reshape(1, 256),
        edge_target.reshape(1, 256),
        weights.reshape(1, 1280),
        update_weight,
        update_bias.reshape(1, 1024),
        pair_ids.T,
        neg_ids.T,
        hidden_weight,
        hidden_bias.reshape(1, 1024),
        score_grad.T,
    )
    embedding, scores, shared_weight, shared_bias, shared_score = hand_over(
        embedding, scores, shared_weight, aux
    )
    return (embedding, scores.T, shared_weight, shared_bias.reshape(8), shared_score.reshape(8))


def solution(mesh):
    return jax.shard_map(
        body,
        mesh=mesh,
        in_specs=(
            P("node", None),
            P(),
            P(),
            P("node"),
            P("node"),
            P("node"),
            P("node"),
            P(),
            P(),
            P(("pair", "node"), None),
            P(("pair", "node"), None),
            P(),
            P(),
            P(),
            P(("pair", "node"), None),
        ),
        out_specs=(
            P("node", None),
            P(("pair", "node"), None),
            P(("pair", "node"), None),
            P(("pair", "node")),
            P(("pair", "node")),
        ),
        check_vma=False,
    )
```

```python
import functools
import jax
import jax.numpy as jnp
from jax import lax
from jax.experimental import pallas as pl
from jax.experimental.pallas import tpu as pltpu
from jax.sharding import PartitionSpec as P

MESH = pl.DeviceIdType.MESH
F32 = jnp.float32
BF16 = jnp.bfloat16
ORDERS = (("z", "x", "y"), ("x", "y", "z"), ("y", "z", "x"))


def place():
    node = lax.axis_index("node")
    return {
        "z": lax.axis_index("pair"),
        "x": node // 8,
        "y": (node // 2) % 4,
        "c": node % 2,
    }


def device(at, **other):
    pos = dict(at, **other)
    return (pos["z"], pos["x"] * 8 + pos["y"] * 2 + pos["c"])


def ring(at, axis, step):
    return device(at, **{axis: (at[axis] + step) % 4})


def part(ref, third, **sel):
    full = pl.ds(0, 4)
    a, b, c = ORDERS[third]
    return ref.at[third, sel.get(a, full), sel.get(b, full), sel.get(c, full)]


def spot(n):
    chip, third = n // 3, n % 3
    at = {"z": chip // 16, "x": (chip // 4) % 4, "y": chip % 4}
    return (third,) + tuple(at[axis] for axis in ORDERS[third])


class Links:
    def __init__(self, send_sem, recv_sem):
        self.send_sem, self.recv_sem, self.copies = send_sem, recv_sem, []
        self.sent = self.received = 0

    def start(self, src, dst, to):
        copy = pltpu.make_async_remote_copy(
            src_ref=src,
            dst_ref=dst,
            send_sem=self.send_sem.at[self.sent],
            recv_sem=self.recv_sem.at[self.received],
            device_id=to,
            device_id_type=MESH,
        )
        copy.start()
        self.sent += 1
        self.received += 1
        self.copies.append(copy)
        return copy

    def drop(self, done):
        self.copies = [copy for copy in self.copies if copy is not done]

    def drain(self):
        for copy in self.copies:
            copy.wait_send()
        self.copies, self.sent = [], 0


def add_into(dst, *srcs):
    if len(srcs) == 1:
        dst[...] = dst[...] + srcs[0][...]
        return
    total = dst[...].astype(F32)
    for src in srcs:
        total = total + src[...].astype(F32)
    dst[...] = total.astype(dst.dtype)


GATHER_UNITS = ((0, 5), (5, 5), (10, 6))


def table(ref, half, units, **sel):
    full = pl.ds(0, 4)
    return ref.at[sel.get("z", full), sel.get("x", full), sel.get("y", full), half, pl.ds(*units)]


def network_kernel(
    feats_ref, mw_hbm, mb_ref, source_ref, slot_ref, target_ref, weights_ref,
    uw_hbm, ub_ref, pair_ref, neg_ref, hw_hbm, hb_ref, sg_in,
    emb_ref, scores_out, gw_ref, aux_out_ref,
    turn, sg_ref, scores_ref,
    mw, uw, hw_ref, outbox, inbox, avg_out, avg_in, rows_f, shared, keys, onehot, grad, q_ref, cand_ref,
    q2t, qt8, gq2, query_act, acc_bias, acc_score,
    own, give, take,
    opp1, near1, opp2, near2, last3, final, final_in,
    aux, aux_core, aux_in,
    load_sem, msg_send, msg_recv, core_send, core_recv, send_sem, recv_sem,
):
    at = place()
    core = at["c"]
    node = lax.axis_index("node")
    sibling = device(at, c=1 - core)
    barrier = pltpu.get_barrier_semaphore()

    def greet(k, carry):
        pl.semaphore_signal(
            barrier, inc=1, device_id=(at["z"], (node + k) % 32), device_id_type=MESH
        )
        return carry

    lax.fori_loop(1, 32, greet, 0)
    for step in (1, 2, 3):
        pl.semaphore_signal(barrier, inc=1, device_id=ring(at, "z", step), device_id_type=MESH)
    links = Links(send_sem, recv_sem)

    quarter = pl.ds(pl.multiple_of(at["z"] * 256, 256), 256)
    load_mw = pltpu.make_async_copy(mw_hbm.at[:, quarter], mw, load_sem.at[0])
    load_uw = pltpu.make_async_copy(uw_hbm, uw, load_sem.at[1])
    load_hw = pltpu.make_async_copy(hw_hbm, hw_ref, load_sem.at[2])
    load_mw.start()

    def pick(cond):
        return jnp.where(cond, 1.0, 0.0).astype(BF16)

    row = lax.broadcasted_iota(jnp.int32, (128, 256), 0)
    weight = weights_ref[:, pl.ds(1024, 256)]
    target = target_ref[...].astype(F32)
    from_node = jnp.where(row == source_ref[...], weight, 0.0)
    beside = jnp.where(row == 0, weight, jnp.where(row == 1, target, 0.0))
    edge_rows = jnp.concatenate([from_node, beside], axis=0).astype(BF16)
    to_slot = pick(lax.broadcasted_iota(jnp.int32, (512, 256), 0) == slot_ref[...])
    routed = lax.dot_general(
        to_slot, edge_rows, (((1,), (1,)), ((), ())), preferred_element_type=F32
    ).astype(BF16)
    load_mw.wait()
    load_uw.start()
    project = jnp.dot(feats_ref[...], mw[...], preferred_element_type=F32) + mb_ref[:, quarter]
    project = jnp.maximum(project, 0.0).astype(BF16)
    message = jnp.dot(routed[:, :128], project, preferred_element_type=F32).astype(BF16)
    outbox[:, :, pl.ds(0, 256)] = message.reshape(32, 16, 256)
    outbox[:, :, pl.ds(256, 128)] = routed[:, 128:].reshape(32, 16, 128)
    pl.semaphore_wait(barrier, 34)

    def message_copy(k):
        to = (node + k) % 32
        return pltpu.make_async_remote_copy(
            src_ref=outbox.at[to],
            dst_ref=inbox.at[node],
            send_sem=msg_send.at[k],
            recv_sem=msg_recv.at[k],
            device_id=(at["z"], to),
            device_id_type=MESH,
        )

    def send_message(k, carry):
        message_copy(k).start()
        return carry

    def wait_message(k, carry):
        message_copy(k).wait_recv()
        return carry

    lax.fori_loop(1, 32, send_message, 0)
    load_hw.start()
    inbox[node] = outbox[node]
    my_rows = pl.ds(pl.multiple_of(at["z"] * 32, 32), 32)
    load_uw.wait()
    rows_f[...] = (
        jnp.dot(feats_ref[my_rows], uw[pl.ds(0, 1024)], preferred_element_type=F32) + ub_ref[...]
    )
    turn[...] = jnp.zeros_like(turn)
    turn[pl.ds(0, 2), pl.ds(0, 64)] = pair_ref[...].astype(F32)
    turn[pl.ds(2, 15), pl.ds(0, 64)] = neg_ref[...].astype(F32)
    turn[pl.ds(32, 16), pl.ds(0, 64)] = sg_in[...]
    turned = turn[...].T[:64]
    sg_ref[...] = turned[:, 32:48]
    ids = turned[:, :17].astype(jnp.int32)
    for k in range(17):
        column = ids[:, k : k + 1]
        key = (
            ((column >> 5) & 3) * 1024 + ((column >> 7) & 1) * 512 + (column >> 8) * 32 + (column & 31)
        )
        keys[pl.ds(k * 64, 64)] = jnp.broadcast_to(key, (64, 128))
    lax.fori_loop(1, 32, wait_message, 0)

    got = inbox[...].reshape(512, 384)
    got_target = got[:, 256:].astype(F32)[:, 1:2]
    lane = lax.broadcasted_iota(jnp.int32, (512, 128), 1).astype(F32)
    to_row = pick(got_target == lane)
    sums = lax.dot_general(to_row, got, (((0,), (0,)), ((), ())), preferred_element_type=F32)
    average = (sums[:, :256] / jnp.maximum(sums[:, 256:257], 1.0)).astype(BF16)
    avg_out[...] = average.reshape(4, 32, 256)
    copies = [
        links.start(avg_out.at[(at["z"] + d) % 4], avg_in.at[at["z"]], ring(at, "z", d))
        for d in (1, 2, 3)
    ]
    avg_in[at["z"]] = avg_out[at["z"]]
    for copy in copies:
        copy.wait_recv()
    rect = rows_f[...]
    for k in range(4):
        rect = rect + jnp.dot(
            avg_in[k], uw[pl.ds(1024 + k * 256, 256)], preferred_element_type=F32
        )
    rect = jnp.maximum(rect, 0.0)
    scale = lax.rsqrt(jnp.mean(rect * rect, axis=1, keepdims=True) + 1e-06)
    emb = (rect * scale).astype(BF16)

    chip = {"z": at["z"], "x": at["x"], "y": at["y"]}
    for half in range(2):
        for t in range(4):
            for h in range(2):
                shared[at["z"], at["x"], at["y"], half, core * 8 + t * 2 + h] = emb[
                    h * 16 : (h + 1) * 16, half * 512 + t * 128 : half * 512 + (t + 1) * 128
                ]
    mine_units = (core * 8, 8)
    crossing = table(shared, 1 - core, mine_units, **chip)
    keeping = table(shared, core, mine_units, **chip)
    arrivals = [links.start(crossing, crossing, sibling)]
    arrivals.append(links.start(keeping, keeping, sibling))
    arrivals[0].wait_recv()

    def pass_on(view, to):
        return links.start(view, view, to)

    low, high = pl.ds(0, 2), pl.ds(2, 2)
    held = lambda p, **sel: table(shared, core, GATHER_UNITS[p], **sel)
    first = []
    for p in range(3):
        a = ORDERS[p][0]
        first.append([pass_on(held(p, **chip), ring(at, a, d)) for d in (1, 2, 3)])

    def both_ways(p, axis, halved, **sel):
        me = {axis: at[axis]}
        right, left = ring(at, axis, 1), ring(at, axis, 3)
        lower = held(p, **sel, **me, **{halved: low})
        upper = held(p, **sel, **me, **{halved: high})
        return [pass_on(lower, right), pass_on(upper, left), pass_on(upper, right), pass_on(lower, left)]

    def forward_halves(p, axis, halved, copies, **sel):
        left, right = {axis: (at[axis] + 3) % 4}, {axis: (at[axis] + 1) % 4}
        copies[0].wait_recv()
        copies.append(pass_on(held(p, **sel, **left, **{halved: low}), ring(at, axis, 1)))
        copies[1].wait_recv()
        copies.append(pass_on(held(p, **sel, **right, **{halved: high}), ring(at, axis, 3)))

    def share_sides(p, axis, copies, **sel):
        for k, step in ((2, 3), (3, 1)):
            copies[k].wait_recv()
            arrivals.append(
                pass_on(held(p, **sel, **{axis: (at[axis] + step) % 4}), sibling)
            )

    def last_halves(p, axis, copies, **sel):
        copies[4].wait_recv()
        copies[5].wait_recv()

    def far_view(p, axis, **sel):
        return held(p, **sel, **{axis: (at[axis] + 2) % 4})

    second = []
    for p in range(3):
        a, b, c = ORDERS[p]
        for d in (1, 2, 3):
            first[p][d - 1].wait_recv()
        second.append(both_ways(p, b, a, **{c: at[c]}))
        for d in (1, 2, 3):
            arrivals.append(
                pass_on(held(p, **{a: (at[a] + d) % 4, b: at[b], c: at[c]}), sibling)
            )
    for p in range(3):
        a, b, c = ORDERS[p]
        forward_halves(p, b, a, second[p], **{c: at[c]})
    for p in range(3):
        a, b, c = ORDERS[p]
        share_sides(p, b, second[p], **{c: at[c]})
    third = []
    for p in range(3):
        a, b, c = ORDERS[p]
        last_halves(p, b, second[p])
        third.append(both_ways(p, c, a))
        arrivals.append(pass_on(far_view(p, b, **{c: at[c]}), sibling))
    def pick_rows(k, carry):
        start = pl.multiple_of(k * 128, 128)
        lanes = lax.broadcasted_iota(jnp.int32, (1088, 128), 1) + start
        onehot[:, pl.ds(start, 128)] = pick(keys[...] == lanes)
        return carry

    lax.fori_loop(0, 32, pick_rows, 0)
    for p in range(3):
        a, b, c = ORDERS[p]
        forward_halves(p, c, a, third[p])
    for p in range(3):
        a, b, c = ORDERS[p]
        share_sides(p, c, third[p])
    for p in range(3):
        a, b, c = ORDERS[p]
        last_halves(p, c, third[p])
        arrivals.append(pass_on(far_view(p, c), sibling))
    for copy in arrivals[1:]:
        copy.wait_recv()

    for z in range(4):
        for half in range(2):
            for t in range(4):
                emb_ref[pl.ds(z * 32, 32), pl.ds(half * 512 + t * 128, 128)] = shared[
                    z, at["x"], at["y"], half, pl.ds(core * 8 + t * 2, 2)
                ].reshape(32, 128)

    def fetch(n, carry):
        half, pair = n // 2, n % 2
        tiles = []
        for t in range(2):
            tiles.append(
                jnp.concatenate(
                    [
                        shared[z, :, :, half, pl.ds(s * 8 + pair * 4 + t * 2, 2)].reshape(512, 128)
                        for z in range(4)
                        for s in (0, 1)
                    ],
                    axis=0,
                )
            )
        cols = pl.ds(pl.multiple_of(n * 256, 256), 256)
        rows = jnp.dot(
            onehot[...], jnp.concatenate(tiles, axis=1), preferred_element_type=F32
        ).astype(BF16)
        q_ref[:, cols] = rows[:64]
        cand_ref[:, cols] = rows[64:]
        return carry

    lax.fori_loop(0, 4, fetch, 0)
    load_hw.wait()

    links.drain()
    candt, prodt = uw.at[pl.ds(0, 1024)], uw.at[pl.ds(1024, 1024)]
    query_t = q_ref[...].T
    q2t[...] = jnp.concatenate([query_t, query_t], axis=1)
    qt8[...] = jnp.concatenate([query_t] * 8, axis=1)
    query_act[...] = jnp.dot(q_ref[...], hw_ref[pl.ds(0, 1024)], preferred_element_type=F32) + hb_ref[...]
    acc_bias[...] = jnp.zeros_like(acc_bias)
    acc_score[...] = jnp.zeros_like(acc_score)
    scores_ref[...] = jnp.zeros_like(scores_ref)

    def forward(i, query_grad):
        rows = pl.ds(pl.multiple_of(i * 512, 512), 512)
        cand = cand_ref[rows]
        product = (cand.reshape(8, 64, 1024) * q_ref[...][None]).reshape(512, 1024)
        act = jnp.dot(cand, hw_ref[pl.ds(1024, 1024)], preferred_element_type=F32)
        act = act + jnp.dot(product, hw_ref[pl.ds(2048, 1024)], preferred_element_type=F32)
        flipped = cand.T
        candt[:, rows] = flipped
        prodt[:, rows] = flipped * qt8[...]
        sw = weights_ref[:, pl.ds(0, 1024)]
        sg = sg_ref[...]
        lane = lax.broadcasted_iota(jnp.int32, (64, 16), 1)
        score = scores_ref[...]
        bias_sum = acc_bias[...]
        score_sum = acc_score[...]
        for k in range(8):
            mine = lane == i * 8 + k
            x = act[k * 64 : (k + 1) * 64] + query_act[...]
            s = 0.5 * jnp.tanh(0.5 * x) + 0.5
            hidden = (x * s).astype(BF16).astype(F32)
            score = score + jnp.where(mine, jnp.sum(hidden * sw, axis=1, keepdims=True), 0.0)
            cot = jnp.sum(jnp.where(mine, sg, 0.0), axis=1, keepdims=True)
            score_sum = score_sum + jnp.sum((cot * hidden).reshape(8, 8, 1024), axis=0)
            pre_grad = (cot * sw * s * (1.0 + x * (1.0 - s))).astype(BF16)
            grad[pl.ds(pl.multiple_of(i * 512 + k * 64, 64), 64)] = pre_grad
            pre_grad = pre_grad.astype(F32)
            bias_sum = bias_sum + jnp.sum(pre_grad.reshape(8, 8, 1024), axis=0)
            query_grad = query_grad + pre_grad
        scores_ref[...] = score
        acc_bias[...] = bias_sum
        acc_score[...] = score_sum
        return query_grad

    query_grad = lax.fori_loop(0, 2, forward, jnp.zeros((64, 1024), F32))
    high = query_grad.astype(BF16)
    gq2[pl.ds(0, 64)] = high
    gq2[pl.ds(64, 64)] = (query_grad - high.astype(F32)).astype(BF16)
    aux[pl.ds(0, 1)] = jnp.sum(acc_bias[...], axis=0, keepdims=True)
    aux[pl.ds(1, 1)] = jnp.sum(acc_score[...], axis=0, keepdims=True)
    aux_core_copy = links.start(aux, aux_core, sibling)

    def core_copy(n, j):
        return pltpu.make_async_remote_copy(
            src_ref=give.at[n, j],
            dst_ref=take.at[n, j],
            send_sem=core_send.at[n * 6 + j],
            recv_sem=core_recv.at[n * 6 + j],
            device_id=sibling,
            device_id_type=MESH,
        )

    def chunk(n, j, xt_ref, g_ref, k):
        x = xt_ref[pl.ds(pl.multiple_of(k * 512, 512), 512), :]
        cols = pl.ds(pl.multiple_of((1 - core) * 512 + n * 256, 256), 256)
        other = jnp.dot(x, g_ref[:, cols], preferred_element_type=F32)
        give[n, j] = other.astype(BF16).reshape(32, 16, 256)
        core_copy(n, j).start()
        cols = pl.ds(pl.multiple_of(core * 512 + n * 256, 256), 256)
        mine = jnp.dot(x, g_ref[:, cols], preferred_element_type=F32).astype(BF16)
        for b in range(32):
            own[(n,) + spot(j * 32 + b)] = mine[b * 16 : (b + 1) * 16]

    def land(n, j):
        core_copy(n, j).wait_recv()
        for b in range(32):
            to = (n,) + spot(j * 32 + b)
            own[to] = own[to] + take[n, j, b]

    def loop(body):
        for k in range(2):
            body(k)

    def step_c(n):
        def run(k):
            chunk(n, k + 2, candt, grad, k)
            if n == 1:
                land(0, k)

        loop(run)

    def step_p(n):
        def run(k):
            chunk(n, k + 4, prodt, grad, k)
            land(n, k + 2)

        loop(run)

    def step_q(n):
        def run(k):
            chunk(n, k, q2t, gq2, k)
            land(n, k + 4)

        loop(run)

    my_cols = pl.ds(pl.multiple_of(core * 512, 512), 512)
    other_cols = pl.ds(pl.multiple_of((1 - core) * 512, 512), 512)

    low, high_half = pl.ds(0, 2), pl.ds(2, 2)

    def aux_start(stage):
        axis = ("x", "y", "z")[stage]
        return [
            links.start(aux, aux_in.at[stage * 3 + d - 1], ring(at, axis, d)) for d in (1, 2, 3)
        ]

    def aux_add(stage, copies):
        for copy in copies:
            copy.wait()
            links.drop(copy)
        add_into(aux, *[aux_in.at[stage * 3 + d - 1] for d in (1, 2, 3)])

    def first_sends(view, opp, near, axis):
        me = at[axis]
        right, left = ring(at, axis, 1), ring(at, axis, 3)
        far = (me + 2) % 4
        a = links.start(view(far, high_half), opp.at[0], right)
        b = links.start(view(far, low), opp.at[1], left)
        c = links.start(view((me + 1) % 4, low), near.at[0, low], right)
        d = links.start(view((me + 3) % 4, high_half), near.at[1, high_half], left)
        return [a, b, c, d]

    def second_sends(view, opp, near, axis, copies):
        me = at[axis]
        right, left = ring(at, axis, 1), ring(at, axis, 3)
        copies[0].wait_recv()
        add_into(view((me + 1) % 4, high_half), opp.at[0])
        copies.append(links.start(view((me + 1) % 4, high_half), near.at[0, high_half], right))
        copies[1].wait_recv()
        add_into(view((me + 3) % 4, low), opp.at[1])
        copies.append(links.start(view((me + 3) % 4, low), near.at[1, low], left))

    def finish(view, near, axis, copies):
        for copy in copies[2:]:
            copy.wait_recv()
        add_into(view(at[axis], pl.ds(0, 4)), near.at[0], near.at[1])

    def view1(n, third):
        a, b, _ = ORDERS[third]
        return lambda i, h: part(own.at[n], third, **{a: i, b: h})

    def view2(n, third):
        a, b, c = ORDERS[third]
        return lambda i, h: part(own.at[n], third, **{a: at[a], b: i, c: h})

    def stage1_first(n):
        return [first_sends(view1(n, t), opp1.at[n, t], near1.at[n, t], ORDERS[t][0]) for t in range(3)]

    def stage1_second(n, copies):
        for t in range(3):
            second_sends(view1(n, t), opp1.at[n, t], near1.at[n, t], ORDERS[t][0], copies[t])

    def stage2_first(n, copies):
        sent = []
        for t in range(3):
            finish(view1(n, t), near1.at[n, t], ORDERS[t][0], copies[t])
            sent.append(first_sends(view2(n, t), opp2.at[n, t], near2.at[n, t], ORDERS[t][1]))
        return sent

    def stage2_second(n, copies):
        for t in range(3):
            second_sends(view2(n, t), opp2.at[n, t], near2.at[n, t], ORDERS[t][1], copies[t])

    def stage3(n, copies):
        sent = []
        for t in range(3):
            finish(view2(n, t), near2.at[n, t], ORDERS[t][1], copies[t])
            a, b, c = ORDERS[t]
            sent.append(
                [
                    links.start(
                        part(own.at[n], t, **{a: at[a], b: at[b], c: (at[c] + d) % 4}),
                        last3.at[n, t, d - 1],
                        ring(at, c, d),
                    )
                    for d in (1, 2, 3)
                ]
            )
        return sent

    def total(n, copies):
        for t in range(3):
            value = part(own.at[n], t, z=at["z"], x=at["x"], y=at["y"])[...].astype(F32)
            for d in (1, 2, 3):
                copies[t][d - 1].wait_recv()
                value = value + last3[n, t, d - 1].astype(F32)
            final[pl.ds(t * 16, 16), pl.ds(n * 256, 256)] = value

    step_c(0)
    step_p(0)
    step_q(0)
    step_c(1)
    left_1 = stage1_first(0)
    aux_core_copy.wait()
    links.drop(aux_core_copy)
    add_into(aux, aux_core)
    small = aux_start(0)
    step_p(1)
    stage1_second(0, left_1)
    step_q(1)
    left_2 = stage2_first(0, left_1)
    loop(lambda k: land(1, k))
    right_1 = stage1_first(1)
    aux_add(0, small)
    small = aux_start(1)
    stage2_second(0, left_2)
    stage1_second(1, right_1)
    left_3 = stage3(0, left_2)
    right_2 = stage2_first(1, right_1)
    aux_add(1, small)
    small = aux_start(2)
    stage2_second(1, right_2)
    total(0, left_3)
    right_3 = stage3(1, right_2)
    total(1, right_3)
    swap = links.start(final.at[pl.ds(pl.multiple_of((1 - core) * 24, 8), 24)], final_in, sibling)
    gw_ref[:, my_cols] = final[pl.ds(pl.multiple_of(core * 24, 8), 24)]

    aux_add(2, small)
    index = at["z"] * 32 + node
    near = aux[:, pl.ds(pl.multiple_of(index // 16 * 128, 128), 128)]
    aux_out_ref[...] = pltpu.roll(near, (16 - index % 16) * 8 % 128, axis=1)
    turn[pl.ds(0, 64), pl.ds(0, 16)] = scores_ref[...]
    scores_out[...] = turn[...].T[:16, :64]
    swap.wait_recv()
    gw_ref[:, other_cols] = final_in[...]
    lax.fori_loop(0, 6, lambda j, carry: (core_copy(0, j).wait_send(), core_copy(1, j).wait_send(), carry)[2], 0)
    links.drain()
    lax.fori_loop(1, 32, lambda k, carry: (message_copy(k).wait_send(), carry)[1], 0)


def network(*args):
    vmem = pl.BlockSpec(memory_space=pltpu.VMEM)
    hbm = pl.BlockSpec(memory_space=pl.ANY)
    return pl.pallas_call(
        network_kernel,
        out_shape=(
            jax.ShapeDtypeStruct((128, 1024), BF16),
            jax.ShapeDtypeStruct((16, 64), F32),
            jax.ShapeDtypeStruct((24, 1024), F32),
            jax.ShapeDtypeStruct((2, 128), F32),
        ),
        in_specs=[vmem, hbm] + [vmem] * 5 + [hbm] + [vmem] * 3 + [hbm] + [vmem] * 2,
        out_specs=(vmem,) * 4,
        scratch_shapes=[
            pltpu.VMEM((128, 128), F32),
            pltpu.VMEM((64, 16), F32),
            pltpu.VMEM((64, 16), F32),
            pltpu.VMEM((1024, 256), BF16),
            pltpu.VMEM((2048, 1024), BF16),
            pltpu.VMEM((3072, 1024), BF16),
            pltpu.VMEM((32, 16, 384), BF16),
            pltpu.VMEM((32, 16, 384), BF16),
            pltpu.VMEM((4, 32, 256), BF16),
            pltpu.VMEM((4, 32, 256), BF16),
            pltpu.VMEM((32, 1024), F32),
            pltpu.VMEM((4, 4, 4, 2, 16, 16, 128), BF16),
            pltpu.VMEM((1088, 128), jnp.int32),
            pltpu.VMEM((1088, 4096), BF16),
            pltpu.VMEM((1024, 1024), BF16),
            pltpu.VMEM((64, 1024), BF16),
            pltpu.VMEM((1024, 1024), BF16),
            pltpu.VMEM((1024, 128), BF16),
            pltpu.VMEM((1024, 512), BF16),
            pltpu.VMEM((128, 1024), BF16),
            pltpu.VMEM((64, 1024), F32),
            pltpu.VMEM((8, 1024), F32),
            pltpu.VMEM((8, 1024), F32),
            pltpu.VMEM((2, 3, 4, 4, 4, 16, 256), BF16),
            pltpu.VMEM((2, 6, 32, 16, 256), BF16),
            pltpu.VMEM((2, 6, 32, 16, 256), BF16),
            pltpu.VMEM((2, 3, 2, 2, 4, 16, 256), BF16),
            pltpu.VMEM((2, 3, 2, 4, 4, 16, 256), BF16),
            pltpu.VMEM((2, 3, 2, 2, 16, 256), BF16),
            pltpu.VMEM((2, 3, 2, 4, 16, 256), BF16),
            pltpu.VMEM((2, 3, 3, 16, 256), BF16),
            pltpu.VMEM((48, 512), F32),
            pltpu.VMEM((24, 512), F32),
            pltpu.VMEM((2, 1024), F32),
            pltpu.VMEM((2, 1024), F32),
            pltpu.VMEM((9, 2, 1024), F32),
            pltpu.SemaphoreType.DMA((3,)),
            pltpu.SemaphoreType.DMA((32,)),
            pltpu.SemaphoreType.DMA((32,)),
            pltpu.SemaphoreType.DMA((12,)),
            pltpu.SemaphoreType.DMA((12,)),
            pltpu.SemaphoreType.DMA((104,)),
            pltpu.SemaphoreType.DMA((192,)),
        ],
        compiler_params=pltpu.CompilerParams(
            collective_id=0, has_side_effects=True, vmem_limit_bytes=60 * 2**20
        ),
        cost_estimate=pl.CostEstimate(flops=22 * 10**9, bytes_accessed=14 * 10**6, transcendentals=10**6),
        name="network",
    )(*args)


def hand_over_kernel(emb, scores, weight, aux, emb_out, scores_out, weight_out, bias_out, score_out):
    emb_out[...] = emb[...]
    scores_out[...] = scores[...]
    weight_out[...] = weight[...]
    bias_out[...] = aux[0:1, 0:8]
    score_out[...] = aux[1:2, 0:8]


def hand_over(*arrays):
    vmem = pl.BlockSpec(memory_space=pltpu.VMEM)
    return pl.pallas_call(
        hand_over_kernel,
        out_shape=(
            jax.ShapeDtypeStruct((128, 1024), BF16),
            jax.ShapeDtypeStruct((16, 64), F32),
            jax.ShapeDtypeStruct((24, 1024), F32),
            jax.ShapeDtypeStruct((1, 8), F32),
            jax.ShapeDtypeStruct((1, 8), F32),
        ),
        in_specs=[vmem] * 4,
        out_specs=(vmem,) * 5,
        compiler_params=pltpu.CompilerParams(vmem_limit_bytes=60 * 2**20),
        name="hand_over",
    )(*arrays)


def body(
    node_feats,
    msg_weight,
    msg_bias,
    edge_source,
    edge_slot,
    edge_target,
    edge_weight,
    update_weight,
    update_bias,
    pair_ids,
    neg_ids,
    hidden_weight,
    hidden_bias,
    score_weight,
    score_grad,
):
    weights = lax.optimization_barrier(
        jnp.concatenate([score_weight.astype(F32), edge_weight.astype(F32)])
    )
    embedding, scores, shared_weight, aux = network(
        node_feats,
        msg_weight,
        msg_bias.reshape(1, 1024),
        edge_source.reshape(1, 256),
        edge_slot.reshape(1, 256),
        edge_target.reshape(1, 256),
        weights.reshape(1, 1280),
        update_weight,
        update_bias.reshape(1, 1024),
        pair_ids.T,
        neg_ids.T,
        hidden_weight,
        hidden_bias.reshape(1, 1024),
        score_grad.T,
    )
    embedding, scores, shared_weight, shared_bias, shared_score = hand_over(
        embedding, scores, shared_weight, aux
    )
    return (embedding, scores.T, shared_weight, shared_bias.reshape(8), shared_score.reshape(8))


def solution(mesh):
    return jax.shard_map(
        body,
        mesh=mesh,
        in_specs=(
            P("node", None),
            P(),
            P(),
            P("node"),
            P("node"),
            P("node"),
            P("node"),
            P(),
            P(),
            P(("pair", "node"), None),
            P(("pair", "node"), None),
            P(),
            P(),
            P(),
            P(("pair", "node"), None),
        ),
        out_specs=(
            P("node", None),
            P(("pair", "node"), None),
            P(("pair", "node"), None),
            P(("pair", "node")),
            P(("pair", "node")),
        ),
        check_vma=False,
    )
```
